128 devices in a mesh: dp: 4 (over z_hi, core), seq: 32 (over z_lo, x, y).
Axes of the slice: x: 4, y: 4, z: 4 (z_hi: 2, z_lo: 2; z = z_hi * 2 + z_lo), core: 2. Of those that a mesh axis runs over, the one named last changes fastest.
Arguments:
- head_inputs: bfloat16 [4, 8192, 8192], P('dp', 'seq'), may hold values from -6 to 6
- write_proj: bfloat16 [4, 8192, 1024], P('dp', 'seq'), may hold values from -6 to 6
- read_projection: bfloat16 [4, 8192, 1024], P('dp', 'seq'), may hold values from -0.5 to 0.5
- step_raw: bfloat16 [4, 8192, 128], P('dp', 'seq'), may hold values from -2 to 12
- output_grad: bfloat16 [4, 8192, 8192], P('dp', 'seq'), may hold values from -1.5 to 1.5
- decay_log: float32 [128], P('seq'), may hold values from -0.7 to 1.4
- step_bias: float32 [128], P('seq'), may hold values from -14 to -2
- skip_gain: float32 [128], P('seq'), may hold values from 0.5 to 1.5
Outputs:
- input_grad: bfloat16 [4, 8192, 8192], P('dp', 'seq')
- write_grad: bfloat16 [4, 8192, 1024], P('dp', 'seq')
- read_grad: bfloat16 [4, 8192, 1024], P('dp', 'seq')
- step_grad: bfloat16 [4, 8192, 128], P('dp', 'seq')
- head_gradients: float32 [3, 128], P(None, 'seq')
The draws below stay inside these ranges and needn't reach their ends.
All inputs are finite; a program needn't handle non-finite values.
Results may differ from the reference program's by a relative error of at most 0.023.
Values may be sent and summed in bfloat16 or wider, within the bound.
A program may use at most 640 MiB of HBM per device.

```python
import math
import jax
import jax.numpy as jnp
from jax import lax

HEADS = 128
HEADDIM = 64
NSTATE = 128
NGROUPS = 8
BLOCK = 256
SEQUENCE_TOKENS = 8192
BATCH = 4


def head_levels(key, skew_power):
    rate_key = jax.random.fold_in(key, 101)
    strength_key = jax.random.fold_in(key, 102)
    spread = jax.random.uniform(rate_key, (HEADS,), jnp.float32)
    low_end = math.log(0.25 / SEQUENCE_TOKENS)
    high_end = math.log(0.05)
    head_step_rates = jnp.exp(low_end + (high_end - low_end) * spread ** skew_power)
    spike_magnitude = jnp.exp(jax.random.uniform(strength_key, (HEADS,), jnp.float32, math.log(0.5), math.log(4.0)))
    return (head_step_rates, spike_magnitude)


def softplus_inverse(target):
    return target + jnp.log(-jnp.expm1(-target))


def draw_decay_log(key, part):
    skew_power = 2.0
    head_step_rates, spike_magnitude = head_levels(key, skew_power)
    return jnp.log(spike_magnitude)


def draw_step_bias(key, part):
    skew_power = 2.0
    head_step_rates, spike_magnitude = head_levels(key, skew_power)
    return softplus_inverse(head_step_rates / spike_magnitude)


def draw_step_raw(key, part):
    own_key = jax.random.fold_in(key, 5)
    skew_power = 2.0
    head_step_rates, spike_magnitude = head_levels(key, skew_power)
    noise_key = jax.random.fold_in(own_key, 1)
    place_key = jax.random.fold_in(own_key, 2)
    shape_all = (BATCH, SEQUENCE_TOKENS, HEADS)
    noise_component = jnp.clip(0.5 * jax.random.normal(noise_key, shape_all, jnp.float32), -2.0, 2.0)
    token_positions = jax.random.randint(place_key, (BATCH, 4, HEADS), 0, SEQUENCE_TOKENS)
    token_offset_index = jnp.arange(SEQUENCE_TOKENS)[None, :, None]
    outlier_rows = jnp.zeros(shape_all, dtype=bool)
    for outlier_count in range(4):
        outlier_rows = outlier_rows | (token_offset_index == token_positions[:, outlier_count, None, :])
    spike_value = softplus_inverse(0.3 / spike_magnitude) - softplus_inverse(head_step_rates / spike_magnitude)
    return jnp.where(outlier_rows, spike_value[None, None, :], noise_component).astype(jnp.bfloat16)


def levels(key, dims, shards, least, top_value):
    factor_of = 1.0
    for position, parts in shards:
        heights = jax.random.uniform(jax.random.fold_in(jax.random.fold_in(key, 6), position), (parts,), jnp.float32, least / len(shards), top_value / len(shards))
        factor_of = factor_of * jnp.repeat(jnp.exp(heights), dims[position] // parts).reshape((-1,) + (1,) * (len(dims) - 1 - position))
    return factor_of


def normal_values(rng, dims, scale, bound, shards=(), kind=jnp.bfloat16):
    loudness = levels(rng, dims, shards, -0.22, 0.18) if shards else 1.0
    drawn = jax.random.normal(rng, dims, jnp.float32) * scale * loudness
    return jnp.minimum(jnp.maximum(drawn, -bound), bound).astype(kind)


def setup_inputs(seed: int = 0) -> dict:
    streams_of = jax.random.split(jax.random.key(seed), 9)
    head_inputs = normal_values(streams_of[0], (BATCH, SEQUENCE_TOKENS, HEADS * HEADDIM), 1.0, 6.0, ((0, 4), (1, 32)))
    write_proj = normal_values(streams_of[1], (BATCH, SEQUENCE_TOKENS, NGROUPS * NSTATE), 1.0, 6.0, ((0, 4), (1, 32)))
    read_projection = normal_values(streams_of[2], (BATCH, SEQUENCE_TOKENS, NGROUPS * NSTATE), NSTATE ** -0.5, 0.5, ((0, 4), (1, 32)))
    step_raw = draw_step_raw(jax.random.fold_in(streams_of[8], 71), 0)
    output_grad = normal_values(streams_of[4], (BATCH, SEQUENCE_TOKENS, HEADS * HEADDIM), 0.25, 1.5, ((0, 4), (1, 32)))
    decay_log = draw_decay_log(jax.random.fold_in(streams_of[8], 71), 0)
    step_bias = draw_step_bias(jax.random.fold_in(streams_of[8], 71), 0)
    skip_gain = jnp.clip(0.5 + 1.0 * jax.random.uniform(streams_of[7], (HEADS,), jnp.float32) ** levels(streams_of[7], (HEADS,), ((0, 32),), -0.2, 0.2), 0.5, 1.5)
    return {"head_inputs": head_inputs, "write_proj": write_proj, "read_projection": read_projection, "step_raw": step_raw, "output_grad": output_grad, "decay_log": decay_log, "step_bias": step_bias, "skip_gain": skip_gain}


HIGH = lax.Precision.HIGHEST
BF = jnp.bfloat16
FL = jnp.float32

def spanned_scan(inputs, writes, readout, step_raw, step_bias, decay_log, skip_gain, start_state, block_len):
    seq_len = inputs.shape[0]
    blocks = seq_len // block_len
    step_size = jax.nn.softplus(step_raw + step_bias)
    decays = step_size * -jnp.exp(decay_log)
    input_blk = inputs.reshape(blocks, block_len, -1)
    write_blk = writes.reshape(blocks, block_len, -1)
    read_blk = readout.reshape(blocks, block_len, -1)
    step_blk = step_size.reshape(blocks, block_len)
    within = jnp.cumsum(decays.reshape(blocks, block_len), axis=1)
    lower_mask = jnp.tril(jnp.ones((block_len, block_len), dtype=bool))
    log_gaps = jnp.where(lower_mask, within[:, :, None] - within[:, None, :], -1e+30)
    raw_scores = jnp.einsum('cin,cjn->cij', read_blk, write_blk, preferred_element_type=FL)
    weights = (raw_scores * jnp.exp(log_gaps) * step_blk[:, None, :]).astype(BF)
    local_out = jnp.einsum('cij,cjp->cip', weights, input_blk, preferred_element_type=FL)
    to_end = jnp.exp(within[:, -1:] - within) * step_blk
    scaled_writes = (write_blk.astype(FL) * to_end[:, :, None]).astype(BF)
    block_states = jnp.einsum('cjn,cjp->cpn', scaled_writes, input_blk, preferred_element_type=FL)
    block_boundaries = jnp.cumsum(jnp.concatenate([jnp.zeros((1,), within.dtype), within[:, -1]]))
    lower_blocks = jnp.tril(jnp.ones((blocks + 1, blocks + 1), dtype=bool))
    carry_decay = jnp.exp(jnp.where(lower_blocks, block_boundaries[:, None] - block_boundaries[None, :], -1e+30))
    stacked = jnp.concatenate([start_state[None], block_states], axis=0)
    carried = jnp.einsum('cd,dpn->cpn', carry_decay, stacked, precision=HIGH)
    carried_b = carried[:-1].astype(BF)
    carried_output = jnp.einsum('cin,cpn->cip', read_blk, carried_b, preferred_element_type=FL) * jnp.exp(within)[:, :, None]
    outputs = (local_out + carried_output).reshape(seq_len, -1) + skip_gain * inputs.astype(FL)
    return (outputs, carried[-1])

def head_backward(inputs, writes, readout, step_raw, output_grad, step_bias, decay_log, skip_gain, start_state, end_grad, block_len):

    def forward(in_rows, write_rows, read_rows, raw_rows, bias_value, decay_value, skip_value, state_value):
        return spanned_scan(in_rows, write_rows, read_rows, raw_rows, bias_value, decay_value, skip_value, state_value, block_len)
    _, pullback = jax.vjp(forward, inputs, writes, readout, step_raw, step_bias, decay_log, skip_gain, start_state)
    return pullback((output_grad, end_grad))

def reference(head_inputs, write_proj, read_projection, step_raw, output_grad, decay_log, step_bias, skip_gain):
    per_group = HEADS // NGROUPS
    zero_state = jnp.zeros((HEADDIM, NSTATE), jnp.float32)

    def one_group(group_index):
        write_group = lax.dynamic_slice_in_dim(write_proj, group_index * NSTATE, NSTATE, 2)
        read_group = lax.dynamic_slice_in_dim(read_projection, group_index * NSTATE, NSTATE, 2)

        def one_head(running_sums, offset):
            head_index = (group_index * per_group + offset).astype(jnp.int32)
            inputs = lax.dynamic_slice_in_dim(head_inputs, head_index * HEADDIM, HEADDIM, 2)
            grad_rows = lax.dynamic_slice_in_dim(output_grad, head_index * HEADDIM, HEADDIM, 2).astype(jnp.float32)
            rate_rows = lax.dynamic_slice_in_dim(step_raw, head_index, 1, 2)[:, :, 0].astype(jnp.float32)
            decay_value = lax.dynamic_index_in_dim(decay_log, head_index, 0, keepdims=False)
            step_shift = lax.dynamic_index_in_dim(step_bias, head_index, 0, keepdims=False)
            skip_scale = lax.dynamic_index_in_dim(skip_gain, head_index, 0, keepdims=False)

            def per_sequence(seq_inputs, seq_writes, seq_reads, seq_rates, seq_grads):
                return head_backward(seq_inputs, seq_writes, seq_reads, seq_rates, seq_grads, step_shift, decay_value, skip_scale, zero_state, zero_state, BLOCK)
            pulled = jax.vmap(per_sequence)(inputs, write_group, read_group, rate_rows, grad_rows)
            running_sums = (running_sums[0] + pulled[1].astype(jnp.float32), running_sums[1] + pulled[2].astype(jnp.float32))
            params = jnp.stack([pulled[5], pulled[4], pulled[6]])
            return (running_sums, (pulled[0].astype(jnp.bfloat16), pulled[3].astype(jnp.bfloat16), params))
        start_sums = (jnp.zeros((BATCH, SEQUENCE_TOKENS, NSTATE), jnp.float32), jnp.zeros((BATCH, SEQUENCE_TOKENS, NSTATE), jnp.float32))
        running_sums, stacked = lax.scan(one_head, start_sums, jnp.arange(per_group, dtype=jnp.int32))
        return (running_sums[0].astype(jnp.bfloat16), running_sums[1].astype(jnp.bfloat16), stacked[0], stacked[1], stacked[2])
    write_all, read_all, input_all, rate_all, param_all = lax.map(one_group, jnp.arange(NGROUPS, dtype=jnp.int32))
    input_grad = input_all.transpose(2, 3, 0, 1, 4).reshape(BATCH, SEQUENCE_TOKENS, HEADS * HEADDIM)
    write_grad = write_all.transpose(1, 2, 0, 3).reshape(BATCH, SEQUENCE_TOKENS, NGROUPS * NSTATE)
    read_grad = read_all.transpose(1, 2, 0, 3).reshape(BATCH, SEQUENCE_TOKENS, NGROUPS * NSTATE)
    step_grad = rate_all.transpose(2, 3, 0, 1).reshape(BATCH, SEQUENCE_TOKENS, HEADS)
    factor = 1.0 / math.sqrt(BATCH * SEQUENCE_TOKENS * HEADDIM)
    head_gradients = lax.optimization_barrier(jnp.sum(param_all, axis=3)).reshape(HEADS, 3).T * factor
    return (input_grad, write_grad, read_grad, step_grad, head_gradients)
```

```python
import functools
import math

import jax
import jax.numpy as jnp
from jax import lax
from jax.experimental import pallas as pl
from jax.experimental.pallas import tpu as pltpu
from jax.sharding import PartitionSpec as P

HEADDIM = 64
NSTATE = 128
BLOCK = 256
HALF = 128
PER_GROUP = 16
PAIRS = 8
GW = PER_GROUP * HEADDIM
MSG = 4 * 128 + 16

BF = jnp.bfloat16
FL = jnp.float32


def dot(a, b):
    return jnp.dot(a, b, preferred_element_type=FL)


def dot_nt(a, b):
    return lax.dot_general(a, b, (((1,), (1,)), ((), ())), preferred_element_type=FL)


def dot_tn(a, b):
    return lax.dot_general(a, b, (((0,), (0,)), ((), ())), preferred_element_type=FL)


def hi_lo(a):
    hi = a.astype(BF)
    return hi, (a - hi.astype(FL)).astype(BF)


def three(a):
    hi, _ = hi_lo(a)
    rest = a - hi.astype(FL)
    mid, low = hi_lo(rest)
    return hi, mid, low


def cat_hi_lo(a):
    return jnp.concatenate(hi_lo(a), axis=1)


def tri_sum(tri, a):
    hi, mid, low = three(a)
    return dot(tri, hi) + dot(tri, mid) + dot(tri, low)


def triangle(upper):
    row = lax.broadcasted_iota(jnp.int32, (BLOCK, BLOCK), 0)
    col = lax.broadcasted_iota(jnp.int32, (BLOCK, BLOCK), 1)
    keep = (col >= row) if upper else (col <= row)
    return jnp.where(keep, 1.0, 0.0).astype(BF)


def spread(g, heads, copies):
    row = lax.broadcasted_iota(jnp.int32, (copies * heads, GW), 0)
    col = lax.broadcasted_iota(jnp.int32, (copies * heads, GW), 1)
    if copies == 2:
        row = jnp.where(row >= heads, row - heads, row)
    return jnp.where(row == g * PER_GROUP + col // HEADDIM, 1.0, 0.0).astype(BF)


def gather_heads(p, sel):
    hi, lo = hi_lo(p)
    return dot_nt(hi, sel) + dot_nt(lo, sel)


def rates(raw, prm):
    v = raw.astype(FL) + prm[0:1]
    e = jnp.exp(-jnp.abs(v))
    small = e * (1.0 - e * (0.5 - e * (1.0 / 3 - e * (0.25 - e * 0.2))))
    step = jnp.maximum(v, 0.0) + jnp.where(e < 0.03125, small, jnp.log(1.0 + e))
    rate = -jnp.exp(prm[1:2])
    decay = rate * step
    within = tri_sum(triangle(False), decay)
    return v, step, rate, decay, within


def phase_one(g, heads, x_ref, dy_ref, w_ref, r_ref, cat_te, cat_ew, last3, sd_ref):
    lanes = pl.ds(pl.multiple_of(g * GW, GW), GW)
    glanes = pl.ds(pl.multiple_of(g * NSTATE, NSTATE), NSTATE)
    sel2 = spread(g, heads, 2)
    xt = (x_ref[:, lanes].astype(FL) * dot(cat_te, sel2)).astype(BF)
    dyw = (dy_ref[:, lanes].astype(FL) * dot(cat_ew, sel2)).astype(BF)
    state = dot_tn(w_ref[:, glanes], xt).astype(BF)
    dcar = dot_tn(r_ref[:, glanes], dyw).astype(BF)
    lx = dot(last3, sel2[:heads]).astype(BF)
    for p in range(PAIRS):
        o, slot = g * (PAIRS // 2) + p // 2, p % 2
        sl = slice(p * 128, p * 128 + 128)
        sd_ref[o, slot * 128 : slot * 128 + 128, :] = state[:, sl]
        sd_ref[o, 256 + slot * 128 : 384 + slot * 128, :] = dcar[:, sl]
    for q in range(PAIRS // 2):
        both = jnp.concatenate([lx[:, q * 256 : q * 256 + 128], lx[:, q * 256 + 128 : q * 256 + 256]], axis=0)
        sd_ref[g * (PAIRS // 2) + q, 512:528, :] = both


def decay_factors(step, within):
    last = within[BLOCK - 1 : BLOCK]
    mid = within[HALF - 1 : HALF]
    to_end = jnp.exp(last - within) * step
    from_start = jnp.exp(within)
    to_mid = jnp.exp(mid - within[:HALF]) * step[:HALF]
    from_mid = jnp.exp(within[HALF:] - mid)
    return last, to_end, from_start, to_mid, from_mid


def last_terms(last):
    h, m, l = three(last)
    return jnp.concatenate([h, m, l, jnp.zeros((5, last.shape[1]), BF)], axis=0)


def kernel_a(heads, groups, x_ref, dy_ref, w_ref, r_ref, raw_ref, prm_ref, sd_ref, te_s, ew_s, l3_s):
    _, step, _, _, within = rates(raw_ref[...], prm_ref[...])
    last, to_end, from_start, _, _ = decay_factors(step, within)
    te_s[...] = cat_hi_lo(to_end)
    ew_s[...] = cat_hi_lo(from_start)
    l3_s[...] = last_terms(last)

    def group(g, _):
        phase_one(g, heads, x_ref, dy_ref, w_ref, r_ref, te_s[...], ew_s[...], l3_s[...], sd_ref)
        return 0

    lax.fori_loop(0, groups, group, 0)


def source_decay(m, d, slot):
    rows = m[d, 512 + 8 * slot : 520 + 8 * slot, :].astype(FL)
    return jnp.exp(rows[0:1] + rows[1:2] + rows[2:3])


def kernel_s(blocks, m_ref, back_ref, cf, gf):
    cf[...] = jnp.zeros_like(cf)
    gf[...] = jnp.zeros_like(gf)

    def scan(i, _):
        for slot in range(2):
            rows = slice(slot * 128, slot * 128 + 128)
            back_ref[i, rows, :] = cf[rows, :].astype(BF)
            cf[rows, :] = cf[rows, :] * source_decay(m_ref, i, slot) + m_ref[i, rows, :].astype(FL)
            d = blocks - 1 - i
            rev = slice(256 + slot * 128, 384 + slot * 128)
            back_ref[d, rev, :] = gf[rows, :].astype(BF)
            gf[rows, :] = gf[rows, :] * source_decay(m_ref, d, slot) + m_ref[d, rev, :].astype(FL)
        return 0

    lax.fori_loop(0, blocks, scan, 0)


def intra(g, heads, x_ref, dy_ref, w_ref, r_ref, within, wt_s, st_s, cat_tm, cat_fm, dxa, pr, pc, sel2):
    lanes = pl.ds(pl.multiple_of(g * GW, GW), GW)
    glanes = pl.ds(pl.multiple_of(g * NSTATE, NSTATE), NSTATE)
    wg, rg = w_ref[:, glanes], r_ref[:, glanes]
    row = lax.broadcasted_iota(jnp.int32, (HALF, HALF), 0)
    col = lax.broadcasted_iota(jnp.int32, (HALF, HALF), 1)
    lower = col <= row
    first = lax.broadcasted_iota(jnp.int32, (HALF, 128), 1) < HEADDIM
    scores = dot_nt(rg, wg)
    tm = dot(cat_tm, sel2)
    x0 = x_ref[:HALF, lanes].astype(FL)
    xt1 = (x0 * tm).astype(BF)
    dy1 = (dy_ref[HALF:, lanes].astype(FL) * dot(cat_fm, sel2)).astype(BF)
    sb = scores[HALF:, :HALF].astype(BF)
    z = dot(sb, xt1)
    yb = dot_tn(sb, dy1)
    ds_low = dot_nt(dy1, xt1)
    pr[:HALF, :] = jnp.zeros((HALF, GW), FL)
    pr[HALF:, :] = dy1.astype(FL) * z
    pc[:HALF, :] = xt1.astype(FL) * yb
    pc[HALF:, :] = jnp.zeros((HALF, GW), FL)
    dxa[:HALF, lanes] = tm * yb
    dxa[HALF:, lanes] = jnp.zeros((HALF, GW), FL)
    wr = pltpu.roll(within, lax.rem(heads - g * PER_GROUP, heads), 1)
    wt = wt_s[pl.ds(pl.multiple_of(g * PER_GROUP, PER_GROUP), PER_GROUP), :]
    st = st_s[pl.ds(pl.multiple_of(g * PER_GROUP, PER_GROUP), PER_GROUP), :]
    ds_diag = []
    for sub in range(2):
        rs = slice(sub * HALF, sub * HALF + HALF)
        sd = jnp.where(lower, scores[rs, rs], 0.0)
        ds = jnp.zeros((HALF, HALF), FL)
        for p in range(PAIRS):
            pls = pl.ds(pl.multiple_of(g * GW + p * 128, 128), 128)
            here = slice(p * 128, p * 128 + 128)
            xp, dyp = x_ref[rs, pls], dy_ref[rs, pls]
            none = jnp.zeros_like(xp)
            xst = jnp.concatenate([jnp.where(first, xp, none), jnp.where(first, none, xp)], axis=0)
            dyst = jnp.concatenate([jnp.where(first, dyp, none), jnp.where(first, none, dyp)], axis=0)
            dw = dot_nt(dyp, xst)
            parts = []
            for k in range(2):
                h = 2 * p + k
                gap = jnp.minimum(wr[rs, h : h + 1] - wt[h : h + 1, rs], 0.0)
                es = jnp.exp(gap) * st[h : h + 1, rs]
                ds += dw[:, k * HALF : k * HALF + HALF] * es
                parts.append((sd * es).astype(BF))
            y = dot(jnp.concatenate(parts, axis=1), xst)
            dxp = dot_tn(jnp.concatenate(parts, axis=0), dyst)
            pr[rs, here] += dyp.astype(FL) * y
            pc[rs, here] += xp.astype(FL) * dxp
            dxa[rs, pls] += dxp
        ds_diag.append(jnp.where(lower, ds, 0.0))
    top = jnp.concatenate([ds_diag[0], jnp.zeros((HALF, HALF), FL)], axis=1)
    low = jnp.concatenate([ds_low, ds_diag[1]], axis=1)
    dscore = jnp.concatenate([top, low], axis=0).astype(BF)
    return dot(dscore, wg), dot_tn(dscore, rg)


def kernel_b(
    heads, groups, x_ref, dy_ref, w_ref, r_ref, raw_ref, prm_ref, sd_ref, cg_ref,
    dx_ref, dw_ref, dr_ref, dstep_ref, hg_ref,
    within_s, step_s, wt_s, st_s, te_s, ew_s, tm_s, fm_s, r_acc, c_acc, dl_acc, sk_acc, dxa, pr, pc,
):
    _, step, _, _, within = rates(raw_ref[...], prm_ref[...])
    last, to_end, from_start, to_mid, from_mid = decay_factors(step, within)
    within_s[...] = within
    step_s[...] = step
    wt_s[...] = within.T
    st_s[...] = step.T
    te_s[...] = cat_hi_lo(to_end)
    ew_s[...] = cat_hi_lo(from_start)
    tm_s[...] = cat_hi_lo(to_mid)
    fm_s[...] = cat_hi_lo(from_mid)
    for acc in (r_acc, c_acc, dl_acc, sk_acc):
        acc[...] = jnp.zeros_like(acc)
    full = jnp.concatenate([jnp.exp(last), prm_ref[2:3], jnp.zeros((6, heads), FL)], axis=0)
    full = cat_hi_lo(full)

    def group(g, _):
        lanes = pl.ds(pl.multiple_of(g * GW, GW), GW)
        glanes = pl.ds(pl.multiple_of(g * NSTATE, NSTATE), NSTATE)
        sel2 = spread(g, heads, 2)
        sel = sel2[:heads]
        dr_i, dw_i = intra(g, heads, x_ref, dy_ref, w_ref, r_ref, within_s[...], wt_s, st_s, tm_s[...], fm_s[...], dxa, pr, pc, sel2)
        xf, dyf = x_ref[:, lanes].astype(FL), dy_ref[:, lanes].astype(FL)
        te = dot(te_s[...], sel2)
        xt = (xf * te).astype(BF)
        dyw = (dyf * dot(ew_s[...], sel2)).astype(BF)
        wide = dot(full, sel2)
        g4 = g * (PAIRS // 2)

        def lane_cat(ref, base):
            return jnp.concatenate(
                [ref[g4 + p // 2, base + (p % 2) * 128 : base + (p % 2) * 128 + 128, :] for p in range(PAIRS)], axis=1
            )

        car, gst, own = lane_cat(cg_ref, 0), lane_cat(cg_ref, 256), lane_cat(sd_ref, 0)
        zc = dot(r_ref[:, glanes], car)
        zg = dot(w_ref[:, glanes], gst)
        pr[...] += dyw.astype(FL) * zc
        pc[...] += xt.astype(FL) * zg
        r_acc[...] += gather_heads(pr[...], sel)
        c_acc[...] += gather_heads(pc[...], sel)
        ends = jnp.sum(gst.astype(FL) * (own.astype(FL) + wide[0:1] * car.astype(FL)), axis=0, keepdims=True)
        skips = jnp.sum(xf * dyf, axis=0, keepdims=True)
        both = jnp.concatenate([ends, skips, jnp.zeros((6, GW), FL)], axis=0)
        both = gather_heads(both, sel)
        dl_acc[...] += both[0:1]
        sk_acc[...] += both[1:2]
        dx_ref[:, lanes] = (dxa[:, lanes] + te * zg + wide[1:2] * dyf).astype(BF)
        dr_ref[:, glanes] = (dr_i + dot_nt(dyw, car)).astype(BF)
        dw_ref[:, glanes] = (dw_i + dot_nt(xt, gst)).astype(BF)
        return 0

    lax.fori_loop(0, groups, group, 0)
    v, step, rate, decay, _ = rates(raw_ref[...], prm_ref[...])
    trow = lax.broadcasted_iota(jnp.int32, (BLOCK, heads), 0)
    dwithin = r_acc[...] - c_acc[...] + jnp.where(trow == BLOCK - 1, dl_acc[...], 0.0)
    dld = tri_sum(triangle(True), dwithin)
    dstep = c_acc[...] / step + rate * dld
    draw = dstep / (1.0 + jnp.exp(-v))
    dstep_ref[...] = draw.astype(BF)
    hg_ref[...] = jnp.concatenate(
        [
            jnp.sum(dld * decay, axis=0, keepdims=True),
            jnp.sum(draw, axis=0, keepdims=True),
            sk_acc[...],
            jnp.zeros((5, heads), FL),
        ],
        axis=0,
    )


def body(head_inputs, write_proj, read_projection, step_raw, output_grad, decay_log, step_bias, skip_gain):
    n = lax.axis_size("seq")
    x, w, r, raw, dy = head_inputs[0], write_proj[0], read_projection[0], step_raw[0], output_grad[0]
    heads = raw.shape[1]
    groups = heads // PER_GROUP
    owned = heads // n
    factor = 1.0 / math.sqrt(lax.axis_size("dp") * n * BLOCK * HEADDIM)
    prm = jnp.stack([step_bias, decay_log, skip_gain])
    prm = lax.all_gather(prm, "seq", axis=1, tiled=True)
    prm = jnp.concatenate([prm, jnp.zeros((5, heads), FL)], axis=0)
    vm = pl.BlockSpec(memory_space=pltpu.VMEM)
    params = pltpu.CompilerParams(vmem_limit_bytes=60 * 2**20)
    cat2 = pltpu.VMEM((BLOCK, 2 * heads), BF)
    cat1 = pltpu.VMEM((HALF, 2 * heads), BF)
    sd = pl.pallas_call(
        functools.partial(kernel_a, heads, groups),
        out_shape=jax.ShapeDtypeStruct((n, MSG, 128), BF),
        in_specs=[vm] * 6,
        out_specs=vm,
        scratch_shapes=[cat2, cat2, pltpu.VMEM((8, heads), BF)],
        compiler_params=params,
        name="block_states",
    )(x, dy, w, r, raw, prm)
    got = lax.all_to_all(sd, "seq", split_axis=0, concat_axis=0, tiled=True)
    back = pl.pallas_call(
        functools.partial(kernel_s, n),
        out_shape=jax.ShapeDtypeStruct((n, 512, 128), BF),
        in_specs=[vm],
        out_specs=vm,
        scratch_shapes=[pltpu.VMEM((256, 128), FL)] * 2,
        compiler_params=params,
        name="state_scan",
    )(got)
    cg = lax.all_to_all(back, "seq", split_axis=0, concat_axis=0, tiled=True)
    full = pltpu.VMEM((BLOCK, heads), FL)
    tr = pltpu.VMEM((heads, BLOCK), FL)
    row = pltpu.VMEM((1, heads), FL)
    wide = pltpu.VMEM((BLOCK, GW), FL)
    dx, dw, dr, dstep, hg = pl.pallas_call(
        functools.partial(kernel_b, heads, groups),
        out_shape=[
            jax.ShapeDtypeStruct(x.shape, BF),
            jax.ShapeDtypeStruct(w.shape, BF),
            jax.ShapeDtypeStruct(r.shape, BF),
            jax.ShapeDtypeStruct(raw.shape, BF),
            jax.ShapeDtypeStruct((8, heads), FL),
        ],
        in_specs=[vm] * 8,
        out_specs=[vm] * 5,
        scratch_shapes=[full, full, tr, tr, cat2, cat2, cat1, cat1, full, full, row, row,
                        pltpu.VMEM((BLOCK, heads * HEADDIM), FL), wide, wide],
        compiler_params=params,
        name="gradients",
    )(x, dy, w, r, raw, prm, sd, cg)
    hg = lax.psum(hg, ("dp", "seq"))
    hg = lax.dynamic_slice_in_dim(hg[:3], lax.axis_index("seq") * owned, owned, 1) * factor
    return (dx[None], dw[None], dr[None], dstep[None], hg)


def solution(mesh):
    tok = P("dp", "seq", None)
    return jax.shard_map(
        body,
        mesh=mesh,
        in_specs=(tok, tok, tok, tok, tok, P("seq"), P("seq"), P("seq")),
        out_specs=(tok, tok, tok, tok, P(None, "seq")),
        check_vma=False,
    )
```

```python
import functools
import math

import jax
import jax.numpy as jnp
from jax import lax
from jax.experimental import pallas as pl
from jax.experimental.pallas import tpu as pltpu
from jax.sharding import PartitionSpec as P

HEADDIM = 64
NSTATE = 128
BLOCK = 256
HALF = 128
PER_GROUP = 16
PAIRS = 8
GW = PER_GROUP * HEADDIM
MSG = 4 * 128 + 16

BF = jnp.bfloat16
FL = jnp.float32
MESH = pl.DeviceIdType.MESH


def dot(a, b):
    return jnp.dot(a, b, preferred_element_type=FL)


def dot_nt(a, b):
    return lax.dot_general(a, b, (((1,), (1,)), ((), ())), preferred_element_type=FL)


def dot_tn(a, b):
    return lax.dot_general(a, b, (((0,), (0,)), ((), ())), preferred_element_type=FL)


def hi_lo(a):
    hi = a.astype(BF)
    return hi, (a - hi.astype(FL)).astype(BF)


def three(a):
    hi, _ = hi_lo(a)
    rest = a - hi.astype(FL)
    mid, low = hi_lo(rest)
    return hi, mid, low


def cat_hi_lo(a):
    return jnp.concatenate(hi_lo(a), axis=1)


def tri_sum(tri, a):
    hi, mid, low = three(a)
    return dot(tri, hi) + dot(tri, mid) + dot(tri, low)


def triangle(upper):
    row = lax.broadcasted_iota(jnp.int32, (BLOCK, BLOCK), 0)
    col = lax.broadcasted_iota(jnp.int32, (BLOCK, BLOCK), 1)
    keep = (col >= row) if upper else (col <= row)
    return jnp.where(keep, 1.0, 0.0).astype(BF)


def spread(g, heads, copies):
    row = lax.broadcasted_iota(jnp.int32, (copies * heads, GW), 0)
    col = lax.broadcasted_iota(jnp.int32, (copies * heads, GW), 1)
    if copies == 2:
        row = jnp.where(row >= heads, row - heads, row)
    return jnp.where(row == g * PER_GROUP + col // HEADDIM, 1.0, 0.0).astype(BF)


def gather_heads(p, sel):
    hi, lo = hi_lo(p)
    return dot_nt(hi, sel) + dot_nt(lo, sel)


def rates(raw, prm):
    v = raw.astype(FL) + prm[0:1]
    e = jnp.exp(-jnp.abs(v))
    small = e * (1.0 - e * (0.5 - e * (1.0 / 3 - e * (0.25 - e * 0.2))))
    step = jnp.maximum(v, 0.0) + jnp.where(e < 0.03125, small, jnp.log(1.0 + e))
    rate = -jnp.exp(prm[1:2])
    decay = rate * step
    within = tri_sum(triangle(False), decay)
    return v, step, rate, decay, within


def phase_one(g, heads, x_ref, dy_ref, w_ref, r_ref, cat_te, cat_ew, last3, sd_ref):
    lanes = pl.ds(pl.multiple_of(g * GW, GW), GW)
    glanes = pl.ds(pl.multiple_of(g * NSTATE, NSTATE), NSTATE)
    sel2 = spread(g, heads, 2)
    xt = (x_ref[:, lanes].astype(FL) * dot(cat_te, sel2)).astype(BF)
    dyw = (dy_ref[:, lanes].astype(FL) * dot(cat_ew, sel2)).astype(BF)
    state = dot_tn(w_ref[:, glanes], xt).astype(BF)
    dcar = dot_tn(r_ref[:, glanes], dyw).astype(BF)
    lx = dot(last3, sel2[:heads]).astype(BF)
    for p in range(PAIRS):
        o, slot = g * (PAIRS // 2) + p // 2, p % 2
        sl = slice(p * 128, p * 128 + 128)
        sd_ref[o, slot * 128 : slot * 128 + 128, :] = state[:, sl]
        sd_ref[o, 256 + slot * 128 : 384 + slot * 128, :] = dcar[:, sl]
    for q in range(PAIRS // 2):
        both = jnp.concatenate([lx[:, q * 256 : q * 256 + 128], lx[:, q * 256 + 128 : q * 256 + 256]], axis=0)
        sd_ref[g * (PAIRS // 2) + q, 512:528, :] = both


def decay_factors(step, within):
    last = within[BLOCK - 1 : BLOCK]
    mid = within[HALF - 1 : HALF]
    to_end = jnp.exp(last - within) * step
    from_start = jnp.exp(within)
    to_mid = jnp.exp(mid - within[:HALF]) * step[:HALF]
    from_mid = jnp.exp(within[HALF:] - mid)
    return last, to_end, from_start, to_mid, from_mid


def last_terms(last):
    h, m, l = three(last)
    return jnp.concatenate([h, m, l, jnp.zeros((5, last.shape[1]), BF)], axis=0)


def source_decay(m, d, slot):
    rows = m[d, 512 + 8 * slot : 520 + 8 * slot, :].astype(FL)
    return jnp.exp(rows[0:1] + rows[1:2] + rows[2:3])


def intra(g, heads, x_ref, dy_ref, w_ref, r_ref, within, wt_s, st_s, cat_tm, cat_fm, dxa, pr, pc, sel2):
    lanes = pl.ds(pl.multiple_of(g * GW, GW), GW)
    glanes = pl.ds(pl.multiple_of(g * NSTATE, NSTATE), NSTATE)
    wg, rg = w_ref[:, glanes], r_ref[:, glanes]
    row = lax.broadcasted_iota(jnp.int32, (HALF, HALF), 0)
    col = lax.broadcasted_iota(jnp.int32, (HALF, HALF), 1)
    lower = col <= row
    first = lax.broadcasted_iota(jnp.int32, (HALF, 128), 1) < HEADDIM
    scores = dot_nt(rg, wg)
    tm = dot(cat_tm, sel2)
    x0 = x_ref[:HALF, lanes].astype(FL)
    xt1 = (x0 * tm).astype(BF)
    dy1 = (dy_ref[HALF:, lanes].astype(FL) * dot(cat_fm, sel2)).astype(BF)
    sb = scores[HALF:, :HALF].astype(BF)
    z = dot(sb, xt1)
    yb = dot_tn(sb, dy1)
    ds_low = dot_nt(dy1, xt1)
    pr[:HALF, :] = jnp.zeros((HALF, GW), FL)
    pr[HALF:, :] = dy1.astype(FL) * z
    pc[:HALF, :] = xt1.astype(FL) * yb
    pc[HALF:, :] = jnp.zeros((HALF, GW), FL)
    dxa[:HALF, lanes] = tm * yb
    dxa[HALF:, lanes] = jnp.zeros((HALF, GW), FL)
    wr = pltpu.roll(within, lax.rem(heads - g * PER_GROUP, heads), 1)
    wt = wt_s[pl.ds(pl.multiple_of(g * PER_GROUP, PER_GROUP), PER_GROUP), :]
    st = st_s[pl.ds(pl.multiple_of(g * PER_GROUP, PER_GROUP), PER_GROUP), :]
    ds_diag = []
    for sub in range(2):
        rs = slice(sub * HALF, sub * HALF + HALF)
        sd = jnp.where(lower, scores[rs, rs], 0.0)
        ds = jnp.zeros((HALF, HALF), FL)
        for p in range(PAIRS):
            pls = pl.ds(pl.multiple_of(g * GW + p * 128, 128), 128)
            here = slice(p * 128, p * 128 + 128)
            xp, dyp = x_ref[rs, pls], dy_ref[rs, pls]
            none = jnp.zeros_like(xp)
            xst = jnp.concatenate([jnp.where(first, xp, none), jnp.where(first, none, xp)], axis=0)
            dyst = jnp.concatenate([jnp.where(first, dyp, none), jnp.where(first, none, dyp)], axis=0)
            dw = dot_nt(dyp, xst)
            parts = []
            for k in range(2):
                h = 2 * p + k
                gap = jnp.minimum(wr[rs, h : h + 1] - wt[h : h + 1, rs], 0.0)
                es = jnp.exp(gap) * st[h : h + 1, rs]
                ds += dw[:, k * HALF : k * HALF + HALF] * es
                parts.append((sd * es).astype(BF))
            y = dot(jnp.concatenate(parts, axis=1), xst)
            dxp = dot_tn(jnp.concatenate(parts, axis=0), dyst)
            pr[rs, here] += dyp.astype(FL) * y
            pc[rs, here] += xp.astype(FL) * dxp
            dxa[rs, pls] += dxp
        ds_diag.append(jnp.where(lower, ds, 0.0))
    top = jnp.concatenate([ds_diag[0], jnp.zeros((HALF, HALF), FL)], axis=1)
    low = jnp.concatenate([ds_low, ds_diag[1]], axis=1)
    dscore = jnp.concatenate([top, low], axis=0).astype(BF)
    return dot(dscore, wg), dot_tn(dscore, rg)


def kernel(
    heads, groups, n, dps, factor,
    x_hbm, dy_hbm, w_hbm, r_hbm, raw_ref, bias_ref, dlog_ref, gain_ref,
    dx_hbm, dw_ref, dr_ref, dstep_ref, hg_ref,
    x_ref, dy_ref, w_ref, r_ref, prm_s, within_s, wt_s, st_s, te_s, ew_s, tm_s, fm_s, l3_s, full_s,
    r_acc, c_acc, dl_acc, sk_acc, dxa, pr, pc, dri, dwi, dxo,
    pg, sd, got, back, cg, cf, hb, hd,
    in_sem, out_sem, pg_s, pg_r, s1, r1, s2, r2, hb_s, hb_r, hd_s, hd_r,
):
    c = lax.axis_index("seq")
    d = lax.axis_index("dp")
    per = PAIRS // 2
    home = c // per
    loads = [
        pltpu.make_async_copy(a, b, in_sem.at[i])
        for i, (a, b) in enumerate(((x_hbm, x_ref), (dy_hbm, dy_ref), (w_hbm, w_ref), (r_hbm, r_ref)))
    ]
    for load in loads:
        load.start()

    barrier = pltpu.get_barrier_semaphore()

    def greet(i, _):
        pl.semaphore_signal(barrier, inc=1, device_id={"seq": lax.rem(c + i, n)}, device_id_type=MESH)
        return 0

    lax.fori_loop(1, n, greet, 0)
    for i in range(1, dps):
        pl.semaphore_signal(barrier, inc=1, device_id={"dp": lax.rem(d + i, dps)}, device_id_type=MESH)
    pl.semaphore_wait(barrier, n - 1 + dps - 1)

    lane = lax.broadcasted_iota(jnp.int32, (8, heads), 1)
    prow = lax.broadcasted_iota(jnp.int32, (8, heads), 0)
    mine = jnp.zeros((8, heads), FL)
    owned = heads // n
    for row, ref in enumerate((bias_ref, dlog_ref, gain_ref)):
        for k in range(owned):
            mine = jnp.where((prow == row) & (lane == c * owned + k), ref[k], mine)
    pg[c] = mine

    def to_all(buf, send, recv, wait):
        def one(t):
            return pltpu.make_async_remote_copy(
                src_ref=buf.at[c], dst_ref=buf.at[c], send_sem=send.at[t], recv_sem=recv.at[c],
                device_id={"seq": t}, device_id_type=MESH,
            )

        def other(t):
            return pltpu.make_async_remote_copy(
                src_ref=buf.at[t], dst_ref=buf.at[t], send_sem=send.at[t], recv_sem=recv.at[t],
                device_id={"seq": t}, device_id_type=MESH,
            )

        def step(i, _):
            t = lax.rem(c + i, n)
            if wait:
                one(t).wait_send()
                other(t).wait_recv()
            else:
                one(t).start()
            return 0

        lax.fori_loop(1, n, step, 0)

    to_all(pg, pg_s, pg_r, False)
    for acc in (r_acc, c_acc, dl_acc, sk_acc):
        acc[...] = jnp.zeros_like(acc)
    to_all(pg, pg_s, pg_r, True)
    prm_s[...] = jnp.sum(pg[...], axis=0)
    _, step, _, _, within = rates(raw_ref[...], prm_s[...])
    last, to_end, from_start, to_mid, from_mid = decay_factors(step, within)
    within_s[...] = within
    wt_s[...] = within.T
    st_s[...] = step.T
    te_s[...] = cat_hi_lo(to_end)
    ew_s[...] = cat_hi_lo(from_start)
    tm_s[...] = cat_hi_lo(to_mid)
    fm_s[...] = cat_hi_lo(from_mid)
    l3_s[...] = last_terms(last)
    full_s[...] = cat_hi_lo(jnp.concatenate([jnp.exp(last), prm_s[2:3], jnp.zeros((6, heads), FL)], axis=0))
    for load in loads:
        load.wait()

    def out(o):
        return pltpu.make_async_remote_copy(
            src_ref=sd.at[o], dst_ref=got.at[c], send_sem=s1.at[o], recv_sem=r1.at[c],
            device_id={"seq": o}, device_id_type=MESH,
        )

    def out_from(t):
        return pltpu.make_async_remote_copy(
            src_ref=sd.at[t], dst_ref=got.at[t], send_sem=s1.at[t], recv_sem=r1.at[t],
            device_id={"seq": t}, device_id_type=MESH,
        )

    def states(i, _):
        g = lax.rem(home + i, groups)
        phase_one(g, heads, x_ref, dy_ref, w_ref, r_ref, te_s[...], ew_s[...], l3_s[...], sd)
        for q in range(per):
            o = g * per + lax.rem(c + q, per)

            @pl.when(o != c)
            def _():
                out(o).start()

        return 0

    lax.fori_loop(0, groups, states, 0)
    got[c] = sd[c]

    def local(g, _):
        glanes = pl.ds(pl.multiple_of(g * NSTATE, NSTATE), NSTATE)
        sel2 = spread(g, heads, 2)
        dr_i, dw_i = intra(
            g, heads, x_ref, dy_ref, w_ref, r_ref, within_s[...], wt_s, st_s, tm_s[...], fm_s[...], dxa, pr, pc, sel2
        )
        dri[:, glanes] = dr_i
        dwi[:, glanes] = dw_i
        r_acc[...] += gather_heads(pr[...], sel2[:heads])
        c_acc[...] += gather_heads(pc[...], sel2[:heads])
        return 0

    lax.fori_loop(0, groups, local, 0)

    def arrived(i, _):
        out_from(lax.rem(c + i, n)).wait_recv()
        return 0

    lax.fori_loop(1, n, arrived, 0)

    def ret(t, half):
        rows = pl.ds(half * 256, 256)
        return pltpu.make_async_remote_copy(
            src_ref=back.at[t, rows], dst_ref=cg.at[c, rows], send_sem=s2.at[half, t], recv_sem=r2.at[half, c],
            device_id={"seq": t}, device_id_type=MESH,
        )

    def ret_from(t, half):
        rows = pl.ds(half * 256, 256)
        return pltpu.make_async_remote_copy(
            src_ref=back.at[t, rows], dst_ref=cg.at[t, rows], send_sem=s2.at[half, t], recv_sem=r2.at[half, t],
            device_id={"seq": t}, device_id_type=MESH,
        )

    for half in range(2):
        cf[...] = jnp.zeros_like(cf)

        def scan(i, _):
            t = i if half == 0 else n - 1 - i
            for slot in range(2):
                rows = slice(slot * 128, slot * 128 + 128)
                mrows = slice(half * 256 + slot * 128, half * 256 + slot * 128 + 128)
                back[t, mrows, :] = cf[rows, :].astype(BF)
                cf[rows, :] = cf[rows, :] * source_decay(got, t, slot) + got[t, mrows, :].astype(FL)
            return 0

        lax.fori_loop(0, n, scan, 0)

        def give(i, _):
            g = lax.rem(home + i // per, groups)
            t = g * per + lax.rem(c + i, per)

            @pl.when(t != c)
            def _():
                ret(t, half).start()

            return 0

        lax.fori_loop(0, n, give, 0)
        cg[c, half * 256 : half * 256 + 256, :] = back[c, half * 256 : half * 256 + 256, :]

    def carried(i, _):
        g = lax.rem(home + groups - i, groups)
        g4 = g * per
        for q in range(per):
            @pl.when(g4 + q != c)
            def _():
                ret_from(g4 + q, 0).wait_recv()
                ret_from(g4 + q, 1).wait_recv()

        lanes = pl.ds(pl.multiple_of(g * GW, GW), GW)
        glanes = pl.ds(pl.multiple_of(g * NSTATE, NSTATE), NSTATE)
        sel2 = spread(g, heads, 2)
        sel = sel2[:heads]
        xf, dyf = x_ref[:, lanes].astype(FL), dy_ref[:, lanes].astype(FL)
        te = dot(te_s[...], sel2)
        xt = (xf * te).astype(BF)
        dyw = (dyf * dot(ew_s[...], sel2)).astype(BF)
        wide = dot(full_s[...], sel2)

        def lane_cat(ref, base):
            return jnp.concatenate(
                [ref[g4 + p // 2, base + (p % 2) * 128 : base + (p % 2) * 128 + 128, :] for p in range(PAIRS)], axis=1
            )

        car, gst, own = lane_cat(cg, 0), lane_cat(cg, 256), lane_cat(sd, 0)
        zc = dot(r_ref[:, glanes], car)
        zg = dot(w_ref[:, glanes], gst)
        r_acc[...] += gather_heads(dyw.astype(FL) * zc, sel)
        c_acc[...] += gather_heads(xt.astype(FL) * zg, sel)
        ends = jnp.sum(gst.astype(FL) * (own.astype(FL) + wide[0:1] * car.astype(FL)), axis=0, keepdims=True)
        skips = jnp.sum(xf * dyf, axis=0, keepdims=True)
        both = jnp.concatenate([ends, skips, jnp.zeros((6, GW), FL)], axis=0)
        both = gather_heads(both, sel)
        dl_acc[...] += both[0:1]
        sk_acc[...] += both[1:2]
        dxo[:, lanes] = (dxa[:, lanes] + te * zg + wide[1:2] * dyf).astype(BF)
        pltpu.make_async_copy(dxo.at[:, lanes], dx_hbm.at[:, lanes], out_sem.at[g]).start()
        dr_ref[:, glanes] = (dri[:, glanes] + dot_nt(dyw, car)).astype(BF)
        dw_ref[:, glanes] = (dwi[:, glanes] + dot_nt(xt, gst)).astype(BF)
        return 0

    lax.fori_loop(0, groups, carried, 0)
    v, step, rate, decay, _ = rates(raw_ref[...], prm_s[...])
    trow = lax.broadcasted_iota(jnp.int32, (BLOCK, heads), 0)
    dwithin = r_acc[...] - c_acc[...] + jnp.where(trow == BLOCK - 1, dl_acc[...], 0.0)
    dld = tri_sum(triangle(True), dwithin)
    dstep = c_acc[...] / step + rate * dld
    draw = dstep / (1.0 + jnp.exp(-v))
    hb[c] = jnp.concatenate(
        [
            jnp.sum(dld * decay, axis=0, keepdims=True),
            jnp.sum(draw, axis=0, keepdims=True),
            sk_acc[...],
            jnp.zeros((5, heads), FL),
        ],
        axis=0,
    )
    to_all(hb, hb_s, hb_r, False)
    dstep_ref[...] = draw.astype(BF)
    to_all(hb, hb_s, hb_r, True)
    hd[d] = jnp.sum(hb[...], axis=0)

    def across(j, who):
        return pltpu.make_async_remote_copy(
            src_ref=hd.at[who], dst_ref=hd.at[who], send_sem=hd_s.at[j], recv_sem=hd_r.at[who],
            device_id={"dp": lax.rem(d + j, dps)}, device_id_type=MESH,
        )

    for j in range(1, dps):
        across(j, d).start()

    def leave(t, _):
        @pl.when(t != c)
        def _():
            out(t).wait_send()
            ret(t, 0).wait_send()
            ret(t, 1).wait_send()

        return 0

    lax.fori_loop(0, n, leave, 0)
    for j in range(1, dps):
        across(j, d).wait_send()
        across(j, lax.rem(d + j, dps)).wait_recv()
    total = jnp.sum(hd[...], axis=0) * factor
    hg_ref[...] = pltpu.roll(total, lax.rem(heads - c * owned, heads), 1)

    def written(g, _):
        lanes = pl.ds(pl.multiple_of(g * GW, GW), GW)
        pltpu.make_async_copy(dxo.at[:, lanes], dx_hbm.at[:, lanes], out_sem.at[g]).wait()
        return 0

    lax.fori_loop(0, groups, written, 0)


def body(head_inputs, write_proj, read_projection, step_raw, output_grad, decay_log, step_bias, skip_gain):
    n, dps = lax.axis_size("seq"), lax.axis_size("dp")
    x, w, r, raw, dy = head_inputs[0], write_proj[0], read_projection[0], step_raw[0], output_grad[0]
    heads = raw.shape[1]
    groups = heads // PER_GROUP
    owned = heads // n
    factor = 1.0 / math.sqrt(dps * n * BLOCK * HEADDIM)
    vm = pl.BlockSpec(memory_space=pltpu.VMEM)
    sm = pl.BlockSpec(memory_space=pltpu.SMEM)
    hbm = pl.BlockSpec(memory_space=pl.ANY)
    cat2 = pltpu.VMEM((BLOCK, 2 * heads), BF)
    cat1 = pltpu.VMEM((HALF, 2 * heads), BF)
    full = pltpu.VMEM((BLOCK, heads), FL)
    tr = pltpu.VMEM((heads, BLOCK), FL)
    row = pltpu.VMEM((1, heads), FL)
    wide = pltpu.VMEM((BLOCK, GW), FL)
    small = pltpu.VMEM((n, 8, heads), FL)
    sem = pltpu.SemaphoreType.DMA
    dx, dw, dr, dstep, hg = pl.pallas_call(
        functools.partial(kernel, heads, groups, n, dps, factor),
        out_shape=[
            jax.ShapeDtypeStruct(x.shape, BF),
            jax.ShapeDtypeStruct(w.shape, BF),
            jax.ShapeDtypeStruct(r.shape, BF),
            jax.ShapeDtypeStruct(raw.shape, BF),
            jax.ShapeDtypeStruct((8, heads), FL),
        ],
        in_specs=[hbm] * 4 + [vm] + [sm] * 3,
        out_specs=[hbm] + [vm] * 4,
        scratch_shapes=[
            pltpu.VMEM(x.shape, BF), pltpu.VMEM(x.shape, BF), pltpu.VMEM(w.shape, BF), pltpu.VMEM(r.shape, BF),
            pltpu.VMEM((8, heads), FL), full, tr, tr, cat2, cat2, cat1, cat1,
            pltpu.VMEM((8, heads), BF), pltpu.VMEM((8, 2 * heads), BF),
            full, full, row, row,
            pltpu.VMEM(x.shape, FL), wide, wide, pltpu.VMEM(r.shape, FL), pltpu.VMEM(w.shape, FL), pltpu.VMEM(x.shape, BF),
            small, pltpu.VMEM((n, MSG, 128), BF), pltpu.VMEM((n, MSG, 128), BF),
            pltpu.VMEM((n, 512, 128), BF), pltpu.VMEM((n, 512, 128), BF), pltpu.VMEM((256, 128), FL),
            small, pltpu.VMEM((dps, 8, heads), FL),
            sem((4,)), sem((groups,)), sem((n,)), sem((n,)), sem((n,)), sem((n,)), sem((2, n)), sem((2, n)),
            sem((n,)), sem((n,)), sem((dps,)), sem((dps,)),
        ],
        compiler_params=pltpu.CompilerParams(
            collective_id=0, has_side_effects=True, vmem_limit_bytes=60 * 2**20
        ),
        name="mixer_backward",
    )(x, dy, w, r, raw, step_bias, decay_log, skip_gain)
    return (dx[None], dw[None], dr[None], dstep[None], hg[:3, :owned])


def solution(mesh):
    tok = P("dp", "seq", None)
    return jax.shard_map(
        body,
        mesh=mesh,
        in_specs=(tok, tok, tok, tok, tok, P("seq"), P("seq"), P("seq")),
        out_specs=(tok, tok, tok, tok, P(None, "seq")),
        check_vma=False,
    )
```

```python
import functools
import math

import jax
import jax.numpy as jnp
from jax import lax
from jax.experimental import pallas as pl
from jax.experimental.pallas import tpu as pltpu
from jax.sharding import PartitionSpec as P

HEADDIM = 64
NSTATE = 128
BLOCK = 256
HALF = 128
PER_GROUP = 16
PAIRS = 8
GW = PER_GROUP * HEADDIM
REV = 2 * 128 + 16
MSG = REV + 2 * 128

BF = jnp.bfloat16
FL = jnp.float32
MESH = pl.DeviceIdType.MESH


def dot(a, b):
    return jnp.dot(a, b, preferred_element_type=FL)


def dot_nt(a, b):
    return lax.dot_general(a, b, (((1,), (1,)), ((), ())), preferred_element_type=FL)


def dot_tn(a, b):
    return lax.dot_general(a, b, (((0,), (0,)), ((), ())), preferred_element_type=FL)


def hi_lo(a):
    hi = a.astype(BF)
    return hi, (a - hi.astype(FL)).astype(BF)


def three(a):
    hi, _ = hi_lo(a)
    rest = a - hi.astype(FL)
    mid, low = hi_lo(rest)
    return hi, mid, low


def cat_hi_lo(a):
    return jnp.concatenate(hi_lo(a), axis=1)


def tri_sum(tri, a):
    hi, mid, low = three(a)
    return dot(tri, hi) + dot(tri, mid) + dot(tri, low)


def triangle(upper):
    row = lax.broadcasted_iota(jnp.int32, (BLOCK, BLOCK), 0)
    col = lax.broadcasted_iota(jnp.int32, (BLOCK, BLOCK), 1)
    keep = (col >= row) if upper else (col <= row)
    return jnp.where(keep, 1.0, 0.0).astype(BF)


def spread(g, heads, copies):
    row = lax.broadcasted_iota(jnp.int32, (copies * heads, GW), 0)
    col = lax.broadcasted_iota(jnp.int32, (copies * heads, GW), 1)
    if copies == 2:
        row = jnp.where(row >= heads, row - heads, row)
    return jnp.where(row == g * PER_GROUP + col // HEADDIM, 1.0, 0.0).astype(BF)


def gather_heads(p, sel):
    hi, lo = hi_lo(p)
    return dot_nt(hi, sel) + dot_nt(lo, sel)


def rates(raw, prm):
    v = raw.astype(FL) + prm[0:1]
    e = jnp.exp(-jnp.abs(v))
    small = e * (1.0 - e * (0.5 - e * (1.0 / 3 - e * (0.25 - e * 0.2))))
    step = jnp.maximum(v, 0.0) + jnp.where(e < 0.03125, small, jnp.log(1.0 + e))
    rate = -jnp.exp(prm[1:2])
    decay = rate * step
    within = tri_sum(triangle(False), decay)
    return v, step, rate, decay, within


def decay_factors(step, within):
    last = within[BLOCK - 1 : BLOCK]
    mid = within[HALF - 1 : HALF]
    to_end = jnp.exp(last - within) * step
    from_start = jnp.exp(within)
    to_mid = jnp.exp(mid - within[:HALF]) * step[:HALF]
    from_mid = jnp.exp(within[HALF:] - mid)
    return last, to_end, from_start, to_mid, from_mid


def last_terms(last):
    h, m, l = three(last)
    return jnp.concatenate([h, m, l, jnp.zeros((5, last.shape[1]), BF)], axis=0)


def half_states(g, which, rows_ref, cat, proj_ref, sel2, sd_ref):
    lanes = pl.ds(pl.multiple_of(g * GW, GW), GW)
    glanes = pl.ds(pl.multiple_of(g * NSTATE, NSTATE), NSTATE)
    scaled = (rows_ref[:, lanes].astype(FL) * dot(cat, sel2)).astype(BF)
    state = dot_tn(proj_ref[:, glanes], scaled).astype(BF)
    base = which * REV
    for p in range(PAIRS):
        at = base + (p % 2) * 128
        sd_ref[g * (PAIRS // 2) + p // 2, at : at + 128, :] = state[:, p * 128 : p * 128 + 128]


def source_decay(m, d, slot):
    rows = m[d, 256 + 8 * slot : 264 + 8 * slot, :].astype(FL)
    return jnp.exp(rows[0:1] + rows[1:2] + rows[2:3])


def flip(a, b):
    return a + b - 2 * a * b


def flip4(a, b):
    return 2 * flip(a // 2, b // 2) + flip(a % 2, b % 2)


def far_first(n):
    def hops(k):
        return k // 16 + (0, 1, 2, 1)[k // 4 % 4] + (0, 1, 2, 1)[k % 4]
    return sorted(range(1, n), key=lambda k: -hops(k))


def intra(g, heads, x_ref, dy_ref, w_ref, r_ref, within, wt_s, st_s, cat_tm, cat_fm, dxa, pr, pc, sel2):
    lanes = pl.ds(pl.multiple_of(g * GW, GW), GW)
    glanes = pl.ds(pl.multiple_of(g * NSTATE, NSTATE), NSTATE)
    wg, rg = w_ref[:, glanes], r_ref[:, glanes]
    row = lax.broadcasted_iota(jnp.int32, (HALF, HALF), 0)
    col = lax.broadcasted_iota(jnp.int32, (HALF, HALF), 1)
    lower = col <= row
    first = lax.broadcasted_iota(jnp.int32, (HALF, 128), 1) < HEADDIM
    scores = dot_nt(rg, wg)
    tm = dot(cat_tm, sel2)
    x0 = x_ref[:HALF, lanes].astype(FL)
    xt1 = (x0 * tm).astype(BF)
    dy1 = (dy_ref[HALF:, lanes].astype(FL) * dot(cat_fm, sel2)).astype(BF)
    sb = scores[HALF:, :HALF].astype(BF)
    z = dot(sb, xt1)
    yb = dot_tn(sb, dy1)
    ds_low = dot_nt(dy1, xt1)
    pr[:HALF, :] = jnp.zeros((HALF, GW), FL)
    pr[HALF:, :] = dy1.astype(FL) * z
    pc[:HALF, :] = xt1.astype(FL) * yb
    pc[HALF:, :] = jnp.zeros((HALF, GW), FL)
    dxa[:HALF, lanes] = tm * yb
    dxa[HALF:, lanes] = jnp.zeros((HALF, GW), FL)
    wr = pltpu.roll(within, lax.rem(heads - g * PER_GROUP, heads), 1)
    wt = wt_s[pl.ds(pl.multiple_of(g * PER_GROUP, PER_GROUP), PER_GROUP), :]
    st = st_s[pl.ds(pl.multiple_of(g * PER_GROUP, PER_GROUP), PER_GROUP), :]
    ds_diag = []
    for sub in range(2):
        rs = slice(sub * HALF, sub * HALF + HALF)
        sd = jnp.where(lower, scores[rs, rs], 0.0)
        ds = jnp.zeros((HALF, HALF), FL)
        for p in range(PAIRS):
            pls = pl.ds(pl.multiple_of(g * GW + p * 128, 128), 128)
            here = slice(p * 128, p * 128 + 128)
            xp, dyp = x_ref[rs, pls], dy_ref[rs, pls]
            none = jnp.zeros_like(xp)
            xst = jnp.concatenate([jnp.where(first, xp, none), jnp.where(first, none, xp)], axis=0)
            dyst = jnp.concatenate([jnp.where(first, dyp, none), jnp.where(first, none, dyp)], axis=0)
            dw = dot_nt(dyp, xst)
            parts = []
            for k in range(2):
                h = 2 * p + k
                gap = jnp.minimum(wr[rs, h : h + 1] - wt[h : h + 1, rs], 0.0)
                es = jnp.exp(gap) * st[h : h + 1, rs]
                ds += dw[:, k * HALF : k * HALF + HALF] * es
                parts.append((sd * es).astype(BF))
            y = dot(jnp.concatenate(parts, axis=1), xst)
            dxp = dot_tn(jnp.concatenate(parts, axis=0), dyst)
            pr[rs, here] += dyp.astype(FL) * y
            pc[rs, here] += xp.astype(FL) * dxp
            dxa[rs, pls] += dxp
        ds_diag.append(jnp.where(lower, ds, 0.0))
    top = jnp.concatenate([ds_diag[0], jnp.zeros((HALF, HALF), FL)], axis=1)
    low = jnp.concatenate([ds_low, ds_diag[1]], axis=1)
    dscore = jnp.concatenate([top, low], axis=0).astype(BF)
    return dot(dscore, wg), dot_tn(dscore, rg)


def kernel(
    heads, groups, n, dps, factor,
    x_hbm, dy_hbm, w_hbm, r_hbm, raw_ref, bias_ref, dlog_ref, gain_ref,
    dx_hbm, dw_ref, dr_ref, dstep_ref, hg_ref,
    x_ref, dy_ref, w_ref, r_ref, prm_s, sel_s, step_s, decay_s, sig_s, within_s, wt_s, st_s, te_s, ew_s, tm_s, fm_s, l3_s, full_s,
    r_acc, c_acc, dl_acc, sk_acc, dxa, pr, pc, dri, dwi, dxo,
    pg, sd, got, back, cg, cf, hb, hd,
    in_sem, out_sem, pg_s, pg_r, s1, r1, s2, r2, hb_s, hb_r, hd_s, hd_r,
):
    c = lax.axis_index("seq")
    d = lax.axis_index("dp")
    per = PAIRS // 2
    loads = [
        pltpu.make_async_copy(a, b, in_sem.at[i])
        for i, (a, b) in enumerate(((x_hbm, x_ref), (dy_hbm, dy_ref), (w_hbm, w_ref), (r_hbm, r_ref)))
    ]
    for load in loads:
        load.start()

    zi, xi, yi = c // 16, c // 4 % 4, c % 4

    def peer(k):
        return flip(zi, k // 16) * 16 + flip4(xi, k // 4 % 4) * 4 + flip4(yi, k % 4)

    order = far_first(n)
    barrier = pltpu.get_barrier_semaphore()
    for k in order:
        pl.semaphore_signal(barrier, inc=1, device_id={"seq": peer(k)}, device_id_type=MESH)
    for i in range(1, dps):
        pl.semaphore_signal(barrier, inc=1, device_id={"dp": lax.rem(d + i, dps)}, device_id_type=MESH)
    for g in range(groups):
        sel_s[g] = spread(g, heads, 2)
    for acc in (r_acc, c_acc, dl_acc, sk_acc):
        acc[...] = jnp.zeros_like(acc)
    pl.semaphore_wait(barrier, n - 1 + dps - 1)

    lane = lax.broadcasted_iota(jnp.int32, (8, heads), 1)
    prow = lax.broadcasted_iota(jnp.int32, (8, heads), 0)
    mine = jnp.zeros((8, heads), FL)
    owned = heads // n
    for row, ref in enumerate((bias_ref, dlog_ref, gain_ref)):
        for k in range(owned):
            mine = jnp.where((prow == row) & (lane == c * owned + k), ref[k], mine)
    pg[c] = mine

    def to_all(buf, send, recv, wait):
        def one(t):
            return pltpu.make_async_remote_copy(
                src_ref=buf.at[c], dst_ref=buf.at[c], send_sem=send.at[t], recv_sem=recv.at[c],
                device_id={"seq": t}, device_id_type=MESH,
            )

        def other(t):
            return pltpu.make_async_remote_copy(
                src_ref=buf.at[t], dst_ref=buf.at[t], send_sem=send.at[t], recv_sem=recv.at[t],
                device_id={"seq": t}, device_id_type=MESH,
            )

        if not wait:
            for k in order:
                one(peer(k)).start()
        else:
            def step(i, _):
                t = lax.rem(c + i, n)
                one(t).wait_send()
                other(t).wait_recv()
                return 0

            lax.fori_loop(1, n, step, 0)

    to_all(pg, pg_s, pg_r, False)
    to_all(pg, pg_s, pg_r, True)
    prm_s[...] = jnp.sum(pg[...], axis=0)
    v, step, _, decay, within = rates(raw_ref[...], prm_s[...])
    step_s[...] = step
    decay_s[...] = decay
    sig_s[...] = 1.0 / (1.0 + jnp.exp(-v))
    last, to_end, from_start, to_mid, from_mid = decay_factors(step, within)
    within_s[...] = within
    wt_s[...] = within.T
    st_s[...] = step.T
    te_s[...] = cat_hi_lo(to_end)
    ew_s[...] = cat_hi_lo(from_start)
    tm_s[...] = cat_hi_lo(to_mid)
    fm_s[...] = cat_hi_lo(from_mid)
    l3_s[...] = last_terms(last)
    full_s[...] = cat_hi_lo(jnp.concatenate([jnp.exp(last), prm_s[2:3], jnp.zeros((6, heads), FL)], axis=0))
    for load in loads:
        load.wait()

    def out(t, half, slot):
        rows = pl.ds(half * REV, MSG - REV if half else REV)
        return pltpu.make_async_remote_copy(
            src_ref=sd.at[t, rows], dst_ref=got.at[slot, rows], send_sem=s1.at[half, t], recv_sem=r1.at[half, slot],
            device_id={"seq": t}, device_id_type=MESH,
        )

    def ret(t, half, slot):
        rows = pl.ds(half * 256, 256)
        return pltpu.make_async_remote_copy(
            src_ref=back.at[t, rows], dst_ref=cg.at[slot, rows], send_sem=s2.at[half, t], recv_sem=r2.at[half, slot],
            device_id={"seq": t}, device_id_type=MESH,
        )

    def row_of(j):
        return flip(zi, j // 4) * 4 + flip4(xi, j % 4)

    def two_rows(i):
        if groups < 8:
            return row_of(2 * i), row_of(2 * i + 1)
        return row_of(i), row_of(4 + (i + 2) % 4)

    def send_rows(i, copy, half):
        ga, gb = two_rows(i)
        for ka, kb in ((1, 3), (2, 0), (3, 1), (0, 2)):
            for g, k in ((ga, ka), (gb, kb)):
                t = g * per + flip4(yi, k)

                @pl.when(t != c)
                def _():
                    copy(t, half, c).start()

    def states(i, _):
        for g in two_rows(i):
            half_states(g, 0, x_ref, te_s[...], w_ref, sel_s[g], sd)
            lx = dot(l3_s[...], sel_s[g, :heads]).astype(BF)
            for q in range(per):
                sd[g * per + q, 256:272, :] = jnp.concatenate(
                    [lx[:, q * 256 : q * 256 + 128], lx[:, q * 256 + 128 : q * 256 + 256]], axis=0
                )
        send_rows(i, out, 0)
        return 0

    def grads(i, _):
        for g in two_rows(i):
            half_states(g, 1, dy_ref, ew_s[...], r_ref, sel_s[g], sd)
        send_rows(i, out, 1)
        return 0

    lax.fori_loop(0, groups // 2, states, 0)
    lax.fori_loop(0, groups // 2, grads, 0)
    got[c] = sd[c]

    def local(g, _):
        glanes = pl.ds(pl.multiple_of(g * NSTATE, NSTATE), NSTATE)
        sel2 = sel_s[g]
        dr_i, dw_i = intra(
            g, heads, x_ref, dy_ref, w_ref, r_ref, within_s[...], wt_s, st_s, tm_s[...], fm_s[...], dxa, pr, pc, sel2
        )
        dri[:, glanes] = dr_i
        dwi[:, glanes] = dw_i
        r_acc[...] += gather_heads(pr[...], sel2[:heads])
        c_acc[...] += gather_heads(pc[...], sel2[:heads])
        return 0

    lax.fori_loop(0, groups, local, 0)

    for half in range(2):

        def arrived(i, _):
            t = lax.rem(c + i, n)
            out(t, half, t).wait_recv()
            return 0

        lax.fori_loop(1, n, arrived, 0)
        cf[...] = jnp.zeros_like(cf)

        def scan(i, _):
            t = i if half == 0 else n - 1 - i
            for slot in range(2):
                rows = slice(slot * 128, slot * 128 + 128)
                src = slice(half * REV + slot * 128, half * REV + slot * 128 + 128)
                dst = slice(half * 256 + slot * 128, half * 256 + slot * 128 + 128)
                back[t, dst, :] = cf[rows, :].astype(BF)
                cf[rows, :] = cf[rows, :] * source_decay(got, t, slot) + got[t, src, :].astype(FL)
            return 0

        lax.fori_loop(0, n, scan, 0)

        def give(i, _):
            send_rows(i, ret, half)
            return 0

        lax.fori_loop(0, groups // 2, give, 0)
        cg[c, half * 256 : half * 256 + 256, :] = back[c, half * 256 : half * 256 + 256, :]

    def lane_cat(ref, g, base):
        return jnp.concatenate(
            [ref[g * per + p // 2, base + (p % 2) * 128 : base + (p % 2) * 128 + 128, :] for p in range(PAIRS)], axis=1
        )

    def landed(g, half):
        for q in range(per):
            t = g * per + q

            @pl.when(t != c)
            def _():
                ret(t, half, t).wait_recv()

    def slices(g):
        return pl.ds(pl.multiple_of(g * GW, GW), GW), pl.ds(pl.multiple_of(g * NSTATE, NSTATE), NSTATE)

    def carried(i, _):
        for g in two_rows(i):
            landed(g, 0)
            lanes, glanes = slices(g)
            sel2 = sel_s[g]
            dyw = (dy_ref[:, lanes].astype(FL) * dot(ew_s[...], sel2)).astype(BF)
            car = lane_cat(cg, g, 0)
            r_acc[...] += gather_heads(dyw.astype(FL) * dot(r_ref[:, glanes], car), sel2[:heads])
            dr_ref[:, glanes] = (dri[:, glanes] + dot_nt(dyw, car)).astype(BF)
        return 0

    lax.fori_loop(0, groups // 2, carried, 0)

    def returned(i, _):
        for g in two_rows(i):
            landed(g, 1)
            lanes, glanes = slices(g)
            sel2 = sel_s[g]
            sel = sel2[:heads]
            xf, dyf = x_ref[:, lanes].astype(FL), dy_ref[:, lanes].astype(FL)
            te = dot(te_s[...], sel2)
            xt = (xf * te).astype(BF)
            wide = dot(full_s[...], sel2)
            car, gst, own = lane_cat(cg, g, 0), lane_cat(cg, g, 256), lane_cat(sd, g, 0)
            zg = dot(w_ref[:, glanes], gst)
            dxo[:, lanes] = (dxa[:, lanes] + te * zg + wide[1:2] * dyf).astype(BF)
            pltpu.make_async_copy(dxo.at[:, lanes], dx_hbm.at[:, lanes], out_sem.at[g]).start()
            c_acc[...] += gather_heads(xt.astype(FL) * zg, sel)
            ends = jnp.sum(gst.astype(FL) * (own.astype(FL) + wide[0:1] * car.astype(FL)), axis=0, keepdims=True)
            skips = jnp.sum(xf * dyf, axis=0, keepdims=True)
            both = gather_heads(jnp.concatenate([ends, skips, jnp.zeros((6, GW), FL)], axis=0), sel)
            dl_acc[...] += both[0:1]
            sk_acc[...] += both[1:2]
            dw_ref[:, glanes] = (dwi[:, glanes] + dot_nt(xt, gst)).astype(BF)
        return 0

    lax.fori_loop(0, groups // 2, returned, 0)
    rate = -jnp.exp(prm_s[1:2])
    trow = lax.broadcasted_iota(jnp.int32, (BLOCK, heads), 0)
    dwithin = r_acc[...] - c_acc[...] + jnp.where(trow == BLOCK - 1, dl_acc[...], 0.0)
    dld = tri_sum(triangle(True), dwithin)
    draw = (c_acc[...] / step_s[...] + rate * dld) * sig_s[...]
    hb[c] = jnp.concatenate(
        [
            jnp.sum(dld * decay_s[...], axis=0, keepdims=True),
            jnp.sum(draw, axis=0, keepdims=True),
            sk_acc[...],
            jnp.zeros((5, heads), FL),
        ],
        axis=0,
    )
    to_all(hb, hb_s, hb_r, False)
    dstep_ref[...] = draw.astype(BF)
    to_all(hb, hb_s, hb_r, True)
    hd[d] = jnp.sum(hb[...], axis=0)

    def across(j, who):
        return pltpu.make_async_remote_copy(
            src_ref=hd.at[who], dst_ref=hd.at[who], send_sem=hd_s.at[j], recv_sem=hd_r.at[who],
            device_id={"dp": lax.rem(d + j, dps)}, device_id_type=MESH,
        )

    for j in range(1, dps):
        across(j, d).start()

    def leave(t, _):
        @pl.when(t != c)
        def _():
            for half in range(2):
                out(t, half, c).wait_send()
                ret(t, half, c).wait_send()

        return 0

    lax.fori_loop(0, n, leave, 0)
    for j in range(1, dps):
        across(j, d).wait_send()
        across(j, lax.rem(d + j, dps)).wait_recv()
    total = jnp.sum(hd[...], axis=0) * factor
    hg_ref[...] = pltpu.roll(total, lax.rem(heads - c * owned, heads), 1)

    def written(g, _):
        lanes = pl.ds(pl.multiple_of(g * GW, GW), GW)
        pltpu.make_async_copy(dxo.at[:, lanes], dx_hbm.at[:, lanes], out_sem.at[g]).wait()
        return 0

    lax.fori_loop(0, groups, written, 0)


def body(head_inputs, write_proj, read_projection, step_raw, output_grad, decay_log, step_bias, skip_gain):
    n, dps = lax.axis_size("seq"), lax.axis_size("dp")
    x, w, r, raw, dy = head_inputs[0], write_proj[0], read_projection[0], step_raw[0], output_grad[0]
    heads = raw.shape[1]
    groups = heads // PER_GROUP
    owned = heads // n
    factor = 1.0 / math.sqrt(dps * n * BLOCK * HEADDIM)
    vm = pl.BlockSpec(memory_space=pltpu.VMEM)
    sm = pl.BlockSpec(memory_space=pltpu.SMEM)
    hbm = pl.BlockSpec(memory_space=pl.ANY)
    cat2 = pltpu.VMEM((BLOCK, 2 * heads), BF)
    cat1 = pltpu.VMEM((HALF, 2 * heads), BF)
    full = pltpu.VMEM((BLOCK, heads), FL)
    tr = pltpu.VMEM((heads, BLOCK), FL)
    row = pltpu.VMEM((1, heads), FL)
    wide = pltpu.VMEM((BLOCK, GW), FL)
    small = pltpu.VMEM((n, 8, heads), FL)
    sem = pltpu.SemaphoreType.DMA
    dx, dw, dr, dstep, hg = pl.pallas_call(
        functools.partial(kernel, heads, groups, n, dps, factor),
        out_shape=[
            jax.ShapeDtypeStruct(x.shape, BF),
            jax.ShapeDtypeStruct(w.shape, BF),
            jax.ShapeDtypeStruct(r.shape, BF),
            jax.ShapeDtypeStruct(raw.shape, BF),
            jax.ShapeDtypeStruct((8, heads), FL),
        ],
        in_specs=[hbm] * 4 + [vm] + [sm] * 3,
        out_specs=[hbm] + [vm] * 4,
        scratch_shapes=[
            pltpu.VMEM(x.shape, BF), pltpu.VMEM(x.shape, BF), pltpu.VMEM(w.shape, BF), pltpu.VMEM(r.shape, BF),
            pltpu.VMEM((8, heads), FL), pltpu.VMEM((groups, 2 * heads, GW), BF), full, full, full,
            full, tr, tr, cat2, cat2, cat1, cat1,
            pltpu.VMEM((8, heads), BF), pltpu.VMEM((8, 2 * heads), BF),
            full, full, row, row,
            pltpu.VMEM(x.shape, FL), wide, wide, pltpu.VMEM(r.shape, FL), pltpu.VMEM(w.shape, FL), pltpu.VMEM(x.shape, BF),
            small, pltpu.VMEM((n, MSG, 128), BF), pltpu.VMEM((n, MSG, 128), BF),
            pltpu.VMEM((n, 512, 128), BF), pltpu.VMEM((n, 512, 128), BF), pltpu.VMEM((256, 128), FL),
            small, pltpu.VMEM((dps, 8, heads), FL),
            sem((4,)), sem((groups,)), sem((n,)), sem((n,)), sem((2, n)), sem((2, n)), sem((2, n)), sem((2, n)),
            sem((n,)), sem((n,)), sem((dps,)), sem((dps,)),
        ],
        compiler_params=pltpu.CompilerParams(
            collective_id=0, has_side_effects=True, vmem_limit_bytes=60 * 2**20
        ),
        name="mixer_backward",
    )(x, dy, w, r, raw, step_bias, decay_log, skip_gain)
    return (dx[None], dw[None], dr[None], dstep[None], hg[:3, :owned])


def solution(mesh):
    tok = P("dp", "seq", None)
    return jax.shard_map(
        body,
        mesh=mesh,
        in_specs=(tok, tok, tok, tok, tok, P("seq"), P("seq"), P("seq")),
        out_specs=(tok, tok, tok, tok, P(None, "seq")),
        check_vma=False,
    )
```

```python
import functools
import math

import jax
import jax.numpy as jnp
from jax import lax
from jax.experimental import pallas as pl
from jax.experimental.pallas import tpu as pltpu
from jax.sharding import PartitionSpec as P

HEADDIM = 64
NSTATE = 128
BLOCK = 256
HALF = 128
PER_GROUP = 16
PAIRS = 8
GW = PER_GROUP * HEADDIM
ROW = 4
DEC = 16
PARTS = 8

BF = jnp.bfloat16
FL = jnp.float32
MESH = pl.DeviceIdType.MESH


def dot(a, b):
    return jnp.dot(a, b, preferred_element_type=FL)


def dot_nt(a, b):
    return lax.dot_general(a, b, (((1,), (1,)), ((), ())), preferred_element_type=FL)


def dot_tn(a, b):
    return lax.dot_general(a, b, (((0,), (0,)), ((), ())), preferred_element_type=FL)


def hi_lo(a):
    hi = a.astype(BF)
    return hi, (a - hi.astype(FL)).astype(BF)


def three(a):
    hi, _ = hi_lo(a)
    rest = a - hi.astype(FL)
    mid, low = hi_lo(rest)
    return hi, mid, low


def cat_hi_lo(a):
    return jnp.concatenate(hi_lo(a), axis=1)


def tri_sum(tri, a):
    hi, mid, low = three(a)
    return dot(tri, hi) + dot(tri, mid) + dot(tri, low)


def triangle(upper):
    row = lax.broadcasted_iota(jnp.int32, (BLOCK, BLOCK), 0)
    col = lax.broadcasted_iota(jnp.int32, (BLOCK, BLOCK), 1)
    keep = (col >= row) if upper else (col <= row)
    return jnp.where(keep, 1.0, 0.0).astype(BF)


def spread(g, heads, copies):
    row = lax.broadcasted_iota(jnp.int32, (copies * heads, GW), 0)
    col = lax.broadcasted_iota(jnp.int32, (copies * heads, GW), 1)
    if copies == 2:
        row = jnp.where(row >= heads, row - heads, row)
    return jnp.where(row == g * PER_GROUP + col // HEADDIM, 1.0, 0.0).astype(BF)


def gather_heads(p, sel):
    hi, lo = hi_lo(p)
    return dot_nt(hi, sel) + dot_nt(lo, sel)


def rates(raw, prm):
    v = raw.astype(FL) + prm[0:1]
    e = jnp.exp(-jnp.abs(v))
    small = e * (1.0 - e * (0.5 - e * (1.0 / 3 - e * (0.25 - e * 0.2))))
    step = jnp.maximum(v, 0.0) + jnp.where(e < 0.03125, small, jnp.log(1.0 + e))
    rate = -jnp.exp(prm[1:2])
    decay = rate * step
    within = tri_sum(triangle(False), decay)
    return v, step, rate, decay, within


def decay_factors(step, within):
    last = within[BLOCK - 1 : BLOCK]
    mid = within[HALF - 1 : HALF]
    to_end = jnp.exp(last - within) * step
    from_start = jnp.exp(within)
    to_mid = jnp.exp(mid - within[:HALF]) * step[:HALF]
    from_mid = jnp.exp(within[HALF:] - mid)
    return last, to_end, from_start, to_mid, from_mid


def last_terms(last):
    h, m, l = three(last)
    return jnp.concatenate([h, m, l, jnp.zeros((DEC - 3, last.shape[1]), BF)], axis=0)


def half_states(g, rows_ref, cat, proj_ref, sel2, out_ref, at, keep):
    lanes = pl.ds(pl.multiple_of(g * GW, GW), GW)
    glanes = pl.ds(pl.multiple_of(g * NSTATE, NSTATE), NSTATE)
    scaled = (rows_ref[:, lanes].astype(FL) * dot(cat, sel2)).astype(BF)
    if keep is not None:
        keep[:, lanes] = scaled
    state = dot_tn(proj_ref[:, glanes], scaled).astype(BF)
    for p in range(PAIRS):
        out_ref[at + (pl.ds(p * 128, 128),)] = state[:, p * 128 : p * 128 + 128]


def intra(g, heads, x_ref, dy_ref, w_ref, r_ref, within, wt_s, st_s, cat_tm, cat_fm, dxa, pr, pc, sel2):
    lanes = pl.ds(pl.multiple_of(g * GW, GW), GW)
    glanes = pl.ds(pl.multiple_of(g * NSTATE, NSTATE), NSTATE)
    wg, rg = w_ref[:, glanes], r_ref[:, glanes]
    row = lax.broadcasted_iota(jnp.int32, (HALF, HALF), 0)
    col = lax.broadcasted_iota(jnp.int32, (HALF, HALF), 1)
    lower = col <= row
    first = lax.broadcasted_iota(jnp.int32, (HALF, 128), 1) < HEADDIM
    scores = dot_nt(rg, wg)
    tm = dot(cat_tm, sel2)
    x0 = x_ref[:HALF, lanes].astype(FL)
    xt1 = (x0 * tm).astype(BF)
    dy1 = (dy_ref[HALF:, lanes].astype(FL) * dot(cat_fm, sel2)).astype(BF)
    sb = scores[HALF:, :HALF].astype(BF)
    z = dot(sb, xt1)
    yb = dot_tn(sb, dy1)
    ds_low = dot_nt(dy1, xt1)
    pr[:HALF, :] = jnp.zeros((HALF, GW), FL)
    pr[HALF:, :] = dy1.astype(FL) * z
    pc[:HALF, :] = xt1.astype(FL) * yb
    pc[HALF:, :] = jnp.zeros((HALF, GW), FL)
    dxa[:HALF, lanes] = tm * yb
    dxa[HALF:, lanes] = jnp.zeros((HALF, GW), FL)
    wr = pltpu.roll(within, lax.rem(heads - g * PER_GROUP, heads), 1)
    wt = wt_s[pl.ds(pl.multiple_of(g * PER_GROUP, PER_GROUP), PER_GROUP), :]
    st = st_s[pl.ds(pl.multiple_of(g * PER_GROUP, PER_GROUP), PER_GROUP), :]
    ds_diag = []
    for sub in range(2):
        rs = slice(sub * HALF, sub * HALF + HALF)
        sd = jnp.where(lower, scores[rs, rs], 0.0)
        ds = jnp.zeros((HALF, HALF), FL)
        for p in range(PAIRS):
            pls = pl.ds(pl.multiple_of(g * GW + p * 128, 128), 128)
            here = slice(p * 128, p * 128 + 128)
            xp, dyp = x_ref[rs, pls], dy_ref[rs, pls]
            none = jnp.zeros_like(xp)
            xst = jnp.concatenate([jnp.where(first, xp, none), jnp.where(first, none, xp)], axis=0)
            dyst = jnp.concatenate([jnp.where(first, dyp, none), jnp.where(first, none, dyp)], axis=0)
            dw = dot_nt(dyp, xst)
            parts = []
            for k in range(2):
                h = 2 * p + k
                gap = jnp.minimum(wr[rs, h : h + 1] - wt[h : h + 1, rs], 0.0)
                es = jnp.exp(gap) * st[h : h + 1, rs]
                ds += dw[:, k * HALF : k * HALF + HALF] * es
                parts.append((sd * es).astype(BF))
            y = dot(jnp.concatenate(parts, axis=1), xst)
            dxp = dot_tn(jnp.concatenate(parts, axis=0), dyst)
            pr[rs, here] += dyp.astype(FL) * y
            pc[rs, here] += xp.astype(FL) * dxp
            dxa[rs, pls] += dxp
        ds_diag.append(jnp.where(lower, ds, 0.0))
    top = jnp.concatenate([ds_diag[0], jnp.zeros((HALF, HALF), FL)], axis=1)
    low = jnp.concatenate([ds_low, ds_diag[1]], axis=1)
    dscore = jnp.concatenate([top, low], axis=0).astype(BF)
    return dot(dscore, wg), dot_tn(dscore, rg)


def kernel(
    heads, groups, n, dps, factor,
    x_hbm, dy_hbm, w_hbm, r_hbm, raw_ref, bias_ref, dlog_ref, gain_ref,
    dx_hbm, dw_ref, dr_ref, dstep_ref, hg_ref,
    x_ref, dy_ref, w_ref, r_ref, prm_s, sel_s, step_s, decay_s, sig_s, within_s, wt_s, st_s, te_s, ew_s, tm_s, fm_s, l3_s, full_s,
    r_acc, c_acc, dl_acc, sk_acc, dxa, pr, pc, dri, dwi, xt_s,
    sd, got, back, cg, es, tb, tgot, cb, crow, py, pr_all, hy, hr, hd,
    in_sem, out_sem, s1, r1, s2, r2, s3, r3, s4, r4, py_s, py_r, pz_s, pz_r, hy_s, hy_r, hr_s, hr_r, hd_s, hd_r,
):
    c = lax.axis_index("seq")
    d = lax.axis_index("dp")
    loads = [
        pltpu.make_async_copy(a, b, in_sem.at[i])
        for i, (a, b) in enumerate(((x_hbm, x_ref), (dy_hbm, dy_ref), (w_hbm, w_ref), (r_hbm, r_ref)))
    ]
    for load in loads:
        load.start()

    y, row, rows = c % ROW, c // ROW, n // ROW
    gq = groups // ROW
    pq = gq * PAIRS
    po = pq // rows

    def in_row(t):
        return {"seq": row * ROW + t}

    def in_column(t):
        return {"seq": t * ROW + y}

    def across(t):
        return {"dp": t}

    barrier = pltpu.get_barrier_semaphore()
    for i in range(1, rows):
        pl.semaphore_signal(barrier, inc=1, device_id=in_column((row + i) % rows), device_id_type=MESH)
    for i in range(1, dps):
        pl.semaphore_signal(barrier, inc=1, device_id=across((d + i) % dps), device_id_type=MESH)
    for i in range(1, ROW):
        pl.semaphore_signal(barrier, inc=1, device_id=in_row((y + i) % ROW), device_id_type=MESH)
    for g in range(groups):
        sel_s[g] = spread(g, heads, 2)
    for acc in (r_acc, c_acc, dl_acc, sk_acc):
        acc[...] = jnp.zeros_like(acc)
    pl.semaphore_wait(barrier, rows - 1 + dps - 1 + ROW - 1)

    lane = lax.broadcasted_iota(jnp.int32, (8, heads), 1)
    which = lax.broadcasted_iota(jnp.int32, (8, heads), 0)
    mine = jnp.zeros((8, heads), FL)
    owned = heads // n
    for i, ref in enumerate((bias_ref, dlog_ref, gain_ref)):
        for k in range(owned):
            mine = jnp.where((which == i) & (lane == c * owned + k), ref[k], mine)

    def total(value, buf, me, count, where, send, recv):
        buf[me] = value

        def copy(i, slot):
            return pltpu.make_async_remote_copy(
                src_ref=buf.at[slot], dst_ref=buf.at[slot], send_sem=send.at[i], recv_sem=recv.at[slot],
                device_id=where((me + i) % count), device_id_type=MESH,
            )

        for i in range(1, count):
            copy(i, me).start()
        for i in range(1, count):
            copy(i, me).wait_send()
            copy(i, (me + i) % count).wait_recv()
        return jnp.sum(buf[...], axis=0)

    mine = total(mine, py, y, ROW, in_row, py_s, py_r)
    prm_s[...] = total(mine, pr_all, row, rows, in_column, pz_s, pz_r)
    v, step, _, decay, within = rates(raw_ref[...], prm_s[...])
    step_s[...] = step
    decay_s[...] = decay
    sig_s[...] = 1.0 / (1.0 + jnp.exp(-v))
    last, to_end, from_start, to_mid, from_mid = decay_factors(step, within)
    within_s[...] = within
    wt_s[...] = within.T
    st_s[...] = step.T
    te_s[...] = cat_hi_lo(to_end)
    ew_s[...] = cat_hi_lo(from_start)
    tm_s[...] = cat_hi_lo(to_mid)
    fm_s[...] = cat_hi_lo(from_mid)
    l3_s[...] = last_terms(last)
    full_s[...] = cat_hi_lo(jnp.concatenate([jnp.exp(last), prm_s[2:3], jnp.zeros((6, heads), FL)], axis=0))
    for load in loads:
        load.wait()

    def span(half, k):
        return pl.ds(k * PAIRS * 128, PAIRS * 128 + (pq * DEC if half == 0 and k == gq - 1 else 0))

    def out(half, k, t, slot):
        at = span(half, k)
        return pltpu.make_async_remote_copy(
            src_ref=sd.at[half, t, at], dst_ref=got.at[half, slot, at],
            send_sem=s1.at[half, k, t], recv_sem=r1.at[half, k, slot], device_id=in_row(t), device_id_type=MESH,
        )

    def make(half, t, k):
        g = t * gq + k
        at = (half, t)
        src = (x_ref, te_s, w_ref) if half == 0 else (dy_ref, ew_s, r_ref)
        half_states(g, src[0], src[1][...], src[2], sel_s[g], sd.at[half, t, pl.ds(k * PAIRS * 128, PAIRS * 128)], (), xt_s if half == 0 else None)
        if half == 0:
            lx = dot(l3_s[...], sel_s[g, :heads]).astype(BF)
            for p in range(PAIRS):
                at = pq * 128 + (k * PAIRS + p) * DEC
                sd[0, t, at : at + DEC, :] = lx[:, p * 128 : p * 128 + 128]

    for half in range(2):
        for k in range(gq):

            def send(i, _):
                t = (y + i) % ROW
                make(half, t, k)
                out(half, k, t, y).start()
                return 0

            lax.fori_loop(1, ROW, send, 0)
        for k in range(gq):
            make(half, y, k)
        got[half, y] = sd[half, y]

    def local(g, _):
        glanes = pl.ds(pl.multiple_of(g * NSTATE, NSTATE), NSTATE)
        sel2 = sel_s[g]
        dr_i, dw_i = intra(
            g, heads, x_ref, dy_ref, w_ref, r_ref, within_s[...], wt_s, st_s, tm_s[...], fm_s[...], dxa, pr, pc, sel2
        )
        lanes = pl.ds(pl.multiple_of(g * GW, GW), GW)
        dyf = dy_ref[:, lanes].astype(FL)
        dxa[:, lanes] += dot(full_s[...], sel2)[1:2] * dyf
        skips = jnp.sum(x_ref[:, lanes].astype(FL) * dyf, axis=0, keepdims=True)
        sk_acc[...] += gather_heads(jnp.broadcast_to(skips, (8, GW)), sel2[:heads])[0:1]
        dri[:, glanes] = dr_i
        dwi[:, glanes] = dw_i
        r_acc[...] += gather_heads(pr[...], sel2[:heads])
        c_acc[...] += gather_heads(pc[...], sel2[:heads])
        return 0

    share = (groups * 5 // 8, groups * 6 // 8, groups * 7 // 8, groups)
    lax.fori_loop(0, share[0], local, 0)

    def arrived(half):
        for k in range(gq):
            for i in range(1, ROW):
                t = (y + i) % ROW
                out(half, k, t, t).wait_recv()

    def whole(p):
        return pl.ds(pl.multiple_of(p * 128, 128), 128)

    def up(half, src, t, slot):
        at = pl.ds(0, po * 128 + (po * DEC if half == 0 else 0))
        return pltpu.make_async_remote_copy(
            src_ref=src.at[half, t, at], dst_ref=tgot.at[half, slot, at],
            send_sem=s3.at[half, t], recv_sem=r3.at[half, slot], device_id=in_column(t), device_id_type=MESH,
        )

    def down(half, t, slot):
        return pltpu.make_async_remote_copy(
            src_ref=cb.at[half, t], dst_ref=crow.at[half, slot],
            send_sem=s4.at[half, t], recv_sem=r4.at[half, slot], device_id=in_column(t), device_id_type=MESH,
        )

    def ret(half, k, t, slot):
        at = pl.ds(pl.multiple_of(k * (PAIRS * 128), PAIRS * 128), PAIRS * 128)
        return pltpu.make_async_remote_copy(
            src_ref=back.at[half, t, at], dst_ref=cg.at[half, slot, at],
            send_sem=s2.at[half, k, t], recv_sem=r2.at[half, k, slot], device_id=in_row(t), device_id_type=MESH,
        )

    def blocks(half):
        return range(ROW) if half == 0 else range(ROW - 1, -1, -1)

    def log_decay(rows3):
        f = rows3.astype(FL)
        return f[0:1] + f[1:2] + f[2:3]

    def row_totals(half):
        arrived(half)

        def one(p, _):
            if half == 0:
                logs = jnp.zeros((1, 128), FL)
                for b in range(ROW):
                    log = log_decay(got[0, b, pl.ds(pl.multiple_of(pq * 128 + p * DEC, DEC), DEC), :])
                    es[b, p] = jnp.broadcast_to(jnp.exp(log), (8, 128))
                    logs += log
                h, m, l = three(logs)
                terms = jnp.concatenate([h, m, l, jnp.zeros((DEC - 3, 128), BF)], axis=0)
                tb[0, p // po, pl.ds(pl.multiple_of(po * 128 + (p % po) * DEC, DEC), DEC), :] = terms
            acc = jnp.zeros((128, 128), FL)
            for b in blocks(half):
                acc = acc * es[b, p, 0:1] + got[half, b, whole(p), :].astype(FL)
            tb[half, p // po, whole(p % po), :] = acc.astype(BF)
            return 0

        lax.fori_loop(0, pq, one, 0)
        for i in range(1, rows):
            up(half, tb, (row + i) % rows, row).start()
        tgot[half, row] = tb[half, row]

    def scan_rows(half):
        for i in range(1, rows):
            t = (row + i) % rows
            up(half, tb, t, t).wait_recv()
        for p in range(po):
            at = slice(p * 128, p * 128 + 128)

            def one(i, acc):
                t = i if half == 0 else rows - 1 - i
                cb[half, t, at, :] = acc.astype(BF)
                e = jnp.exp(log_decay(tgot[0, t, po * 128 + p * DEC : po * 128 + (p + 1) * DEC, :]))
                return acc * e + tgot[half, t, at, :].astype(FL)

            lax.fori_loop(0, rows, one, jnp.zeros((128, 128), FL))
        for i in range(1, rows):
            down(half, (row + i) % rows, row).start()
        crow[half, row] = cb[half, row]

    def scan_blocks(half):
        for i in range(1, rows):
            t = (row + i) % rows
            down(half, t, t).wait_recv()
        for k in range(gq):

            def one(i, _):
                p = k * PAIRS + i
                acc = crow[half, p // po, whole(p % po), :].astype(FL)
                for b in blocks(half):
                    back[half, b, whole(p), :] = acc.astype(BF)
                    acc = acc * es[b, p, 0:1] + got[half, b, whole(p), :].astype(FL)
                return 0

            lax.fori_loop(0, PAIRS, one, 0)
            for i in range(1, ROW):
                ret(half, k, (y + i) % ROW, y).start()
        cg[half, y] = back[half, y]

    row_totals(0)
    lax.fori_loop(share[0], share[1], local, 0)
    scan_rows(0)
    lax.fori_loop(share[1], share[2], local, 0)
    scan_blocks(0)
    row_totals(1)
    lax.fori_loop(share[2], share[3], local, 0)
    scan_rows(1)
    scan_blocks(1)

    def lane_cat(ref, half, t, k):
        return jnp.concatenate(
            [ref[half, t, pl.ds(pl.multiple_of((k * PAIRS + p) * 128, 128), 128), :] for p in range(PAIRS)], axis=1
        )

    def landed(half, k, t):
        @pl.when(t != y)
        def _():
            ret(half, k, t, t).wait_recv()

    def slices(g):
        return pl.ds(pl.multiple_of(g * GW, GW), GW), pl.ds(pl.multiple_of(g * NSTATE, NSTATE), NSTATE)

    def carried(j, _):
        k, t = j // ROW, (y + j) % ROW
        g = t * gq + k
        landed(0, k, t)
        lanes, glanes = slices(g)
        sel2 = sel_s[g]
        dyw = (dy_ref[:, lanes].astype(FL) * dot(ew_s[...], sel2)).astype(BF)
        car = lane_cat(cg, 0, t, k)
        r_acc[...] += gather_heads(dyw.astype(FL) * dot(r_ref[:, glanes], car), sel2[:heads])
        dr_ref[:, glanes] = (dri[:, glanes] + dot_nt(dyw, car)).astype(BF)
        return 0

    lax.fori_loop(0, groups, carried, 0)

    def returned(j, _):
        k, t = j // ROW, (y + j) % ROW
        g = t * gq + k
        landed(1, k, t)
        lanes, glanes = slices(g)
        sel2 = sel_s[g]
        sel = sel2[:heads]
        te = dot(te_s[...], sel2)
        xt = xt_s[:, lanes]
        ea = dot(full_s[...], sel2)[0:1]
        car, gst, own = lane_cat(cg, 0, t, k), lane_cat(cg, 1, t, k), lane_cat(sd, 0, t, k)
        zg = dot(w_ref[:, glanes], gst)
        c_acc[...] += gather_heads(xt.astype(FL) * zg, sel)
        ends = jnp.sum(gst.astype(FL) * (own.astype(FL) + ea * car.astype(FL)), axis=0, keepdims=True)
        dl_acc[...] += gather_heads(jnp.broadcast_to(ends, (8, GW)), sel)[0:1]
        dw_ref[:, glanes] = (dwi[:, glanes] + dot_nt(xt, gst)).astype(BF)
        xt_s[:, lanes] = (dxa[:, lanes] + te * zg).astype(BF)
        pltpu.make_async_copy(xt_s.at[:, lanes], dx_hbm.at[:, lanes], out_sem.at[g]).start()
        return 0

    lax.fori_loop(0, groups, returned, 0)
    rate = -jnp.exp(prm_s[1:2])
    trow = lax.broadcasted_iota(jnp.int32, (BLOCK, heads), 0)
    dwithin = r_acc[...] - c_acc[...] + jnp.where(trow == BLOCK - 1, dl_acc[...], 0.0)
    dld = tri_sum(triangle(True), dwithin)
    draw = (c_acc[...] / step_s[...] + rate * dld) * sig_s[...]
    sums = jnp.concatenate(
        [
            jnp.sum(dld * decay_s[...], axis=0, keepdims=True),
            jnp.sum(draw, axis=0, keepdims=True),
            sk_acc[...],
            jnp.zeros((5, heads), FL),
        ],
        axis=0,
    )
    dstep_ref[...] = draw.astype(BF)
    sums = total(sums, hy, y, ROW, in_row, hy_s, hy_r)
    sums = total(sums, hr, row, rows, in_column, hr_s, hr_r)
    sums = total(sums, hd, d, dps, across, hd_s, hd_r) * factor
    hg_ref[...] = pltpu.roll(sums, lax.rem(heads - c * owned, heads), 1)
    for half in range(2):
        for i in range(1, ROW):
            for k in range(gq):
                out(half, k, (y + i) % ROW, y).wait_send()
                ret(half, k, (y + i) % ROW, y).wait_send()
        for i in range(1, rows):
            up(half, tb, (row + i) % rows, row).wait_send()
            down(half, (row + i) % rows, row).wait_send()

    def written(g, _):
        lanes = pl.ds(pl.multiple_of(g * GW, GW), GW)
        pltpu.make_async_copy(xt_s.at[:, lanes], dx_hbm.at[:, lanes], out_sem.at[g]).wait()
        return 0

    lax.fori_loop(0, groups, written, 0)


def finish(owned, dx_in, dw_in, dr_in, ds_in, hg_in, dx_out, dw_out, dr_out, ds_out, hg_out, dx, dw, dr, ds, sem):
    step = BLOCK // PARTS
    moves = [(dx_in.at[pl.ds(i * step, step)], dx.at[pl.ds(i * step, step)], dx_out.at[pl.ds(i * step, step)]) for i in range(PARTS)]
    moves += [(dw_in, dw, dw_out), (dr_in, dr, dr_out), (ds_in, ds, ds_out)]
    loads = [pltpu.make_async_copy(a, b, sem.at[0, i]) for i, (a, b, _) in enumerate(moves)]
    stores = [pltpu.make_async_copy(b, c, sem.at[1, i]) for i, (_, b, c) in enumerate(moves)]
    for load in loads:
        load.start()
    hg_out[...] = hg_in[:3, :owned]
    for load, store in zip(loads, stores):
        load.wait()
        store.start()
    for store in stores:
        store.wait()


def body(head_inputs, write_proj, read_projection, step_raw, output_grad, decay_log, step_bias, skip_gain):
    n, dps = lax.axis_size("seq"), lax.axis_size("dp")
    x, w, r, raw, dy = head_inputs[0], write_proj[0], read_projection[0], step_raw[0], output_grad[0]
    heads = raw.shape[1]
    groups = heads // PER_GROUP
    owned = heads // n
    factor = 1.0 / math.sqrt(dps * n * BLOCK * HEADDIM)
    vm = pl.BlockSpec(memory_space=pltpu.VMEM)
    sm = pl.BlockSpec(memory_space=pltpu.SMEM)
    hbm = pl.BlockSpec(memory_space=pl.ANY)
    cat2 = pltpu.VMEM((BLOCK, 2 * heads), BF)
    cat1 = pltpu.VMEM((HALF, 2 * heads), BF)
    full = pltpu.VMEM((BLOCK, heads), FL)
    tr = pltpu.VMEM((heads, BLOCK), FL)
    row = pltpu.VMEM((1, heads), FL)
    wide = pltpu.VMEM((BLOCK, GW), FL)
    rows, gq = n // ROW, groups // ROW
    pq = gq * PAIRS
    po = pq // rows

    def small(count):
        return pltpu.VMEM((count, 8, heads), FL)

    sem = pltpu.SemaphoreType.DMA
    dx, dw, dr, dstep, hg = pl.pallas_call(
        functools.partial(kernel, heads, groups, n, dps, factor),
        out_shape=[
            jax.ShapeDtypeStruct(x.shape, BF),
            jax.ShapeDtypeStruct(w.shape, BF),
            jax.ShapeDtypeStruct(r.shape, BF),
            jax.ShapeDtypeStruct(raw.shape, BF),
            jax.ShapeDtypeStruct((8, heads), FL),
        ],
        in_specs=[hbm] * 4 + [vm] + [sm] * 3,
        out_specs=[hbm] + [vm] * 4,
        scratch_shapes=[
            pltpu.VMEM(x.shape, BF), pltpu.VMEM(x.shape, BF), pltpu.VMEM(w.shape, BF), pltpu.VMEM(r.shape, BF),
            pltpu.VMEM((8, heads), FL), pltpu.VMEM((groups, 2 * heads, GW), BF), full, full, full,
            full, tr, tr, cat2, cat2, cat1, cat1,
            pltpu.VMEM((DEC, heads), BF), pltpu.VMEM((8, 2 * heads), BF),
            full, full, row, row,
            pltpu.VMEM(x.shape, FL), wide, wide, pltpu.VMEM(r.shape, FL), pltpu.VMEM(w.shape, FL), pltpu.VMEM(x.shape, BF),
            pltpu.VMEM((2, ROW, pq * 128 + pq * DEC, 128), BF), pltpu.VMEM((2, ROW, pq * 128 + pq * DEC, 128), BF),
            pltpu.VMEM((2, ROW, pq * 128, 128), BF), pltpu.VMEM((2, ROW, pq * 128, 128), BF),
            pltpu.VMEM((ROW, pq, 8, 128), FL),
            pltpu.VMEM((2, rows, po * (128 + DEC), 128), BF), pltpu.VMEM((2, rows, po * (128 + DEC), 128), BF),
            pltpu.VMEM((2, rows, po * 128, 128), BF), pltpu.VMEM((2, rows, po * 128, 128), BF),
            small(ROW), small(rows), small(ROW), small(rows), small(dps),
            sem((4,)), sem((groups,)), sem((2, gq, ROW)), sem((2, gq, ROW)), sem((2, gq, ROW)), sem((2, gq, ROW)),
            sem((2, rows)), sem((2, rows)), sem((2, rows)), sem((2, rows)),
            sem((ROW,)), sem((ROW,)), sem((rows,)), sem((rows,)), sem((ROW,)), sem((ROW,)), sem((rows,)), sem((rows,)),
            sem((dps,)), sem((dps,)),
        ],
        compiler_params=pltpu.CompilerParams(
            collective_id=0, has_side_effects=True, vmem_limit_bytes=60 * 2**20
        ),
        name="mixer_backward",
    )(x, dy, w, r, raw, step_bias, decay_log, skip_gain)
    dx, dw, dr, dstep, hg = pl.pallas_call(
        functools.partial(finish, owned),
        out_shape=[jax.ShapeDtypeStruct(a.shape, BF) for a in (dx, dw, dr, dstep)]
        + [jax.ShapeDtypeStruct((3, owned), FL)],
        in_specs=[hbm] * 4 + [vm],
        out_specs=[hbm] * 4 + [vm],
        scratch_shapes=[pltpu.VMEM(a.shape, BF) for a in (dx, dw, dr, dstep)] + [sem((2, 3 + PARTS))],
        name="results",
    )(dx, dw, dr, dstep, hg)
    return (dx[None], dw[None], dr[None], dstep[None], hg)


def solution(mesh):
    tok = P("dp", "seq", None)
    return jax.shard_map(
        body,
        mesh=mesh,
        in_specs=(tok, tok, tok, tok, tok, P("seq"), P("seq"), P("seq")),
        out_specs=(tok, tok, tok, tok, P(None, "seq")),
        check_vma=False,
    )
```

```python
import functools
import math

import jax
import jax.numpy as jnp
from jax import lax
from jax.experimental import pallas as pl
from jax.experimental.pallas import tpu as pltpu
from jax.sharding import PartitionSpec as P

HEADDIM = 64
NSTATE = 128
BLOCK = 256
HALF = 128
PER_GROUP = 16
PAIRS = 8
GW = PER_GROUP * HEADDIM
ROW = 4
DEC = 16
PARTS = 4

BF = jnp.bfloat16
FL = jnp.float32
MESH = pl.DeviceIdType.MESH


def dot(a, b):
    return jnp.dot(a, b, preferred_element_type=FL)


def dot_nt(a, b):
    return lax.dot_general(a, b, (((1,), (1,)), ((), ())), preferred_element_type=FL)


def dot_tn(a, b):
    return lax.dot_general(a, b, (((0,), (0,)), ((), ())), preferred_element_type=FL)


def hi_lo(a):
    hi = a.astype(BF)
    return hi, (a - hi.astype(FL)).astype(BF)


def three(a):
    hi, _ = hi_lo(a)
    rest = a - hi.astype(FL)
    mid, low = hi_lo(rest)
    return hi, mid, low


def cat_hi_lo(a):
    return jnp.concatenate(hi_lo(a), axis=1)


def tri_sum(tri, a):
    hi, mid, low = three(a)
    return dot(tri, hi) + dot(tri, mid) + dot(tri, low)


def triangle(upper):
    row = lax.broadcasted_iota(jnp.int32, (BLOCK, BLOCK), 0)
    col = lax.broadcasted_iota(jnp.int32, (BLOCK, BLOCK), 1)
    keep = (col >= row) if upper else (col <= row)
    return jnp.where(keep, 1.0, 0.0).astype(BF)


def spread(g, heads):
    row = lax.broadcasted_iota(jnp.int32, (heads, GW), 0)
    col = lax.broadcasted_iota(jnp.int32, (heads, GW), 1)
    return jnp.where(row == g * PER_GROUP + col // HEADDIM, 1.0, 0.0).astype(BF)


def gather_heads(p, sel):
    hi, lo = hi_lo(p)
    return dot_nt(hi, sel) + dot_nt(lo, sel)


def rates(raw, prm):
    v = raw.astype(FL) + prm[0:1]
    e = jnp.exp(-jnp.abs(v))
    small = e * (1.0 - e * (0.5 - e * (1.0 / 3 - e * (0.25 - e * 0.2))))
    step = jnp.maximum(v, 0.0) + jnp.where(e < 0.03125, small, jnp.log(1.0 + e))
    rate = -jnp.exp(prm[1:2])
    decay = rate * step
    within = tri_sum(triangle(False), decay)
    return v, step, rate, decay, within


def last_terms(last):
    h, m, l = three(last)
    return jnp.concatenate([h, m, l, jnp.zeros((DEC - 3, last.shape[1]), BF)], axis=0)


def half_states(g, rows_ref, cat, proj_ref, sel2, out_ref, at, keep):
    lanes = pl.ds(pl.multiple_of(g * GW, GW), GW)
    glanes = pl.ds(pl.multiple_of(g * NSTATE, NSTATE), NSTATE)
    scaled = (rows_ref[:, lanes].astype(FL) * dot(cat, sel2)).astype(BF)
    if keep is not None:
        keep[:, lanes] = scaled
    state = dot_tn(proj_ref[:, glanes], scaled).astype(BF)
    for p in range(PAIRS):
        out_ref[at + (pl.ds(p * 128, 128),)] = state[:, p * 128 : p * 128 + 128]


def intra(g, heads, x_ref, dy_ref, w_ref, r_ref, within, wt_s, st_s, cat_tm, cat_fm, dxa, pr, pc, sel2):
    lanes = pl.ds(pl.multiple_of(g * GW, GW), GW)
    glanes = pl.ds(pl.multiple_of(g * NSTATE, NSTATE), NSTATE)
    wg, rg = w_ref[:, glanes], r_ref[:, glanes]
    row = lax.broadcasted_iota(jnp.int32, (HALF, HALF), 0)
    col = lax.broadcasted_iota(jnp.int32, (HALF, HALF), 1)
    lower = col <= row
    first = lax.broadcasted_iota(jnp.int32, (HALF, 128), 1) < HEADDIM
    scores = dot_nt(rg, wg)
    tm = dot(cat_tm, sel2)
    x0 = x_ref[:HALF, lanes].astype(FL)
    xt1 = (x0 * tm).astype(BF)
    dy1 = (dy_ref[HALF:, lanes].astype(FL) * dot(cat_fm, sel2)).astype(BF)
    sb = scores[HALF:, :HALF].astype(BF)
    z = dot(sb, xt1)
    yb = dot_tn(sb, dy1)
    ds_low = dot_nt(dy1, xt1)
    pr[:HALF, :] = jnp.zeros((HALF, GW), FL)
    pr[HALF:, :] = dy1.astype(FL) * z
    pc[:HALF, :] = xt1.astype(FL) * yb
    pc[HALF:, :] = jnp.zeros((HALF, GW), FL)
    dxa[:HALF, lanes] = tm * yb
    dxa[HALF:, lanes] = jnp.zeros((HALF, GW), FL)
    wr = pltpu.roll(within, lax.rem(heads - g * PER_GROUP, heads), 1)
    wt = wt_s[pl.ds(pl.multiple_of(g * PER_GROUP, PER_GROUP), PER_GROUP), :]
    st = st_s[pl.ds(pl.multiple_of(g * PER_GROUP, PER_GROUP), PER_GROUP), :]
    ds_diag = []
    for sub in range(2):
        rs = slice(sub * HALF, sub * HALF + HALF)
        sd = jnp.where(lower, scores[rs, rs], 0.0)
        ds = jnp.zeros((HALF, HALF), FL)
        for p in range(PAIRS):
            pls = pl.ds(pl.multiple_of(g * GW + p * 128, 128), 128)
            here = slice(p * 128, p * 128 + 128)
            xp, dyp = x_ref[rs, pls], dy_ref[rs, pls]
            none = jnp.zeros_like(xp)
            xst = jnp.concatenate([jnp.where(first, xp, none), jnp.where(first, none, xp)], axis=0)
            dyst = jnp.concatenate([jnp.where(first, dyp, none), jnp.where(first, none, dyp)], axis=0)
            dw = dot_nt(dyp, xst)
            parts = []
            for k in range(2):
                h = 2 * p + k
                gap = jnp.minimum(wr[rs, h : h + 1] - wt[h : h + 1, rs], 0.0)
                es = jnp.exp(gap) * st[h : h + 1, rs]
                ds += dw[:, k * HALF : k * HALF + HALF] * es
                parts.append((sd * es).astype(BF))
            y = dot(jnp.concatenate(parts, axis=1), xst)
            dxp = dot_tn(jnp.concatenate(parts, axis=0), dyst)
            pr[rs, here] += dyp.astype(FL) * y
            pc[rs, here] += xp.astype(FL) * dxp
            dxa[rs, pls] += dxp
        ds_diag.append(jnp.where(lower, ds, 0.0))
    top = jnp.concatenate([ds_diag[0], jnp.zeros((HALF, HALF), FL)], axis=1)
    low = jnp.concatenate([ds_low, ds_diag[1]], axis=1)
    dscore = jnp.concatenate([top, low], axis=0).astype(BF)
    return dot(dscore, wg), dot_tn(dscore, rg)


def kernel(
    heads, groups, n, dps, factor,
    x_hbm, dy_hbm, w_hbm, r_hbm, raw_ref, bias_ref, dlog_ref, gain_ref,
    dx_hbm, dw_ref, dr_ref, dstep_ref, hg_ref,
    x_ref, dy_ref, w_ref, r_ref, prm_s, sel_s, step_s, decay_s, sig_s, within_s, wt_s, st_s, te_s, ew_s, tm_s, fm_s, l3_s, full_s,
    r_acc, c_acc, dl_acc, sk_acc, dxa, pr, pc, dri, dwi, xt_s,
    sd, got, back, cg, es, tb, tgot, cb, crow, py, pr_all, hy, hr,
    in_sem, out_sem, s1, r1, s2, r2, s3, r3, s4, r4, py_s, py_r, pz_s, pz_r, hy_s, hy_r, hr_s, hr_r,
):
    c = lax.axis_index("seq")
    d = lax.axis_index("dp")
    loads = [
        pltpu.make_async_copy(a, b, in_sem.at[i])
        for i, (a, b) in enumerate(((x_hbm, x_ref), (dy_hbm, dy_ref), (w_hbm, w_ref), (r_hbm, r_ref)))
    ]
    for load in loads:
        load.start()

    y, row, rows = c % ROW, c // ROW, n // ROW
    gq = groups // ROW
    pq = gq * PAIRS
    po = pq // rows

    def in_row(t):
        return {"seq": row * ROW + t}

    def in_column(t):
        return {"seq": t * ROW + y}

    def in_cell(t):
        return {"seq": row * ROW + t // dps, "dp": t % dps}

    barrier = pltpu.get_barrier_semaphore()
    for i in range(1, rows):
        pl.semaphore_signal(barrier, inc=1, device_id=in_column((row + i) % rows), device_id_type=MESH)
    cell, at_cell = ROW * dps, y * dps + d
    for i in range(1, cell):
        pl.semaphore_signal(barrier, inc=1, device_id=in_cell((at_cell + i) % cell), device_id_type=MESH)
    for g in range(groups):
        one = spread(g, heads)
        sel_s[g, :heads] = one
        sel_s[g, heads:] = one
    for acc in (r_acc, c_acc, dl_acc, sk_acc):
        acc[...] = jnp.zeros_like(acc)
    pl.semaphore_wait(barrier, rows - 1 + cell - 1)

    lane = lax.broadcasted_iota(jnp.int32, (8, heads), 1)
    which = lax.broadcasted_iota(jnp.int32, (8, heads), 0)
    mine = jnp.zeros((8, heads), FL)
    owned = heads // n
    for i, ref in enumerate((bias_ref, dlog_ref, gain_ref)):
        for k in range(owned):
            mine = jnp.where((which == i) & (lane == c * owned + k), ref[k], mine)

    def total(value, buf, me, count, where, send, recv):
        buf[me] = value

        def copy(i, slot):
            return pltpu.make_async_remote_copy(
                src_ref=buf.at[slot], dst_ref=buf.at[slot], send_sem=send.at[i], recv_sem=recv.at[slot],
                device_id=where((me + i) % count), device_id_type=MESH,
            )

        for i in range(1, count):
            copy(i, me).start()
        for i in range(1, count):
            copy(i, me).wait_send()
            copy(i, (me + i) % count).wait_recv()
        return jnp.sum(buf[...], axis=0)

    mine = total(mine, py, y, ROW, in_row, py_s, py_r)
    prm_s[...] = total(mine, pr_all, row, rows, in_column, pz_s, pz_r)
    v, step, _, decay, within = rates(raw_ref[...], prm_s[...])
    within_s[...] = within
    step_s[...] = step
    decay_s[...] = decay
    sig_s[...] = 1.0 / (1.0 + jnp.exp(-v))
    last = within[BLOCK - 1 : BLOCK]
    te_s[...] = cat_hi_lo(jnp.exp(last - within) * step)
    ew_s[...] = cat_hi_lo(jnp.exp(within))
    l3_s[...] = last_terms(last)

    def rest():
        within, step = within_s[...], step_s[...]
        last, mid = within[BLOCK - 1 : BLOCK], within[HALF - 1 : HALF]
        wt_s[...] = within.T
        st_s[...] = step.T
        tm_s[...] = cat_hi_lo(jnp.exp(mid - within[:HALF]) * step[:HALF])
        fm_s[...] = cat_hi_lo(jnp.exp(within[HALF:] - mid))
        full_s[...] = cat_hi_lo(jnp.concatenate([jnp.exp(last), prm_s[2:3], jnp.zeros((6, heads), FL)], axis=0))

    for load in loads:
        load.wait()

    def span(half, k):
        return pl.ds(k * PAIRS * 128, PAIRS * 128 + (pq * DEC if half == 0 and k == gq - 1 else 0))

    def out(half, k, t, slot):
        at = span(half, k)
        return pltpu.make_async_remote_copy(
            src_ref=sd.at[half, t, at], dst_ref=got.at[half, slot, at],
            send_sem=s1.at[half, k, t], recv_sem=r1.at[half, k, slot], device_id=in_row(t), device_id_type=MESH,
        )

    def make(half, t, k):
        g = t * gq + k
        at = (half, t)
        src = (x_ref, te_s, w_ref) if half == 0 else (dy_ref, ew_s, r_ref)
        half_states(g, src[0], src[1][...], src[2], sel_s[g], sd.at[half, t, pl.ds(k * PAIRS * 128, PAIRS * 128)], (), xt_s if half == 0 else None)
        if half == 0:
            lx = dot(l3_s[...], sel_s[g, :heads]).astype(BF)
            for p in range(PAIRS):
                at = pq * 128 + (k * PAIRS + p) * DEC
                sd[0, t, at : at + DEC, :] = lx[:, p * 128 : p * 128 + 128]

    for half in range(2):
        for k in range(gq):

            def send(i, _):
                t = (y + i) % ROW
                make(half, t, k)
                out(half, k, t, y).start()
                return 0

            lax.fori_loop(1, ROW, send, 0)
        for k in range(gq):
            make(half, y, k)
        got[half, y] = sd[half, y]

    def local(g, _):
        glanes = pl.ds(pl.multiple_of(g * NSTATE, NSTATE), NSTATE)
        sel2 = sel_s[g]
        dr_i, dw_i = intra(
            g, heads, x_ref, dy_ref, w_ref, r_ref, within_s[...], wt_s, st_s, tm_s[...], fm_s[...], dxa, pr, pc, sel2
        )
        lanes = pl.ds(pl.multiple_of(g * GW, GW), GW)
        dyf = dy_ref[:, lanes].astype(FL)
        dxa[:, lanes] += dot(full_s[...], sel2)[1:2] * dyf
        skips = jnp.sum(x_ref[:, lanes].astype(FL) * dyf, axis=0, keepdims=True)
        sk_acc[...] += gather_heads(jnp.broadcast_to(skips, (8, GW)), sel2[:heads])[0:1]
        dri[:, glanes] = dr_i
        dwi[:, glanes] = dw_i
        r_acc[...] += gather_heads(pr[...], sel2[:heads])
        c_acc[...] += gather_heads(pc[...], sel2[:heads])
        return 0

    rest()
    share = (groups * 5 // 8, groups * 6 // 8, groups * 7 // 8, groups)
    lax.fori_loop(0, share[0], local, 0)

    def arrived(half):
        for k in range(gq):
            for i in range(1, ROW):
                t = (y + i) % ROW
                out(half, k, t, t).wait_recv()

    def whole(p):
        return pl.ds(pl.multiple_of(p * 128, 128), 128)

    def up(half, src, t, slot):
        at = pl.ds(0, po * 128 + (po * DEC if half == 0 else 0))
        return pltpu.make_async_remote_copy(
            src_ref=src.at[half, t, at], dst_ref=tgot.at[half, slot, at],
            send_sem=s3.at[half, t], recv_sem=r3.at[half, slot], device_id=in_column(t), device_id_type=MESH,
        )

    def down(half, t, slot):
        return pltpu.make_async_remote_copy(
            src_ref=cb.at[half, t], dst_ref=crow.at[half, slot],
            send_sem=s4.at[half, t], recv_sem=r4.at[half, slot], device_id=in_column(t), device_id_type=MESH,
        )

    def ret(half, k, t, slot):
        at = pl.ds(pl.multiple_of(k * (PAIRS * 128), PAIRS * 128), PAIRS * 128)
        return pltpu.make_async_remote_copy(
            src_ref=back.at[half, t, at], dst_ref=cg.at[half, slot, at],
            send_sem=s2.at[half, k, t], recv_sem=r2.at[half, k, slot], device_id=in_row(t), device_id_type=MESH,
        )

    def blocks(half):
        return range(ROW) if half == 0 else range(ROW - 1, -1, -1)

    def log_decay(rows3):
        f = rows3.astype(FL)
        return f[0:1] + f[1:2] + f[2:3]

    def row_totals(half):
        arrived(half)

        def one(p, _):
            if half == 0:
                logs = jnp.zeros((1, 128), FL)
                for b in range(ROW):
                    log = log_decay(got[0, b, pl.ds(pl.multiple_of(pq * 128 + p * DEC, DEC), DEC), :])
                    es[b, p] = jnp.broadcast_to(jnp.exp(log), (8, 128))
                    logs += log
                h, m, l = three(logs)
                terms = jnp.concatenate([h, m, l, jnp.zeros((DEC - 3, 128), BF)], axis=0)
                tb[0, p // po, pl.ds(pl.multiple_of(po * 128 + (p % po) * DEC, DEC), DEC), :] = terms
            acc = jnp.zeros((128, 128), FL)
            for b in blocks(half):
                acc = acc * es[b, p, 0:1] + got[half, b, whole(p), :].astype(FL)
            tb[half, p // po, whole(p % po), :] = acc.astype(BF)
            return 0

        lax.fori_loop(0, pq, one, 0)
        for i in range(1, rows):
            up(half, tb, (row + i) % rows, row).start()
        tgot[half, row] = tb[half, row]

    def scan_rows(half):
        for i in range(1, rows):
            t = (row + i) % rows
            up(half, tb, t, t).wait_recv()
        for p in range(po):
            at = slice(p * 128, p * 128 + 128)

            def one(i, acc):
                t = i if half == 0 else rows - 1 - i
                cb[half, t, at, :] = acc.astype(BF)
                e = jnp.exp(log_decay(tgot[0, t, po * 128 + p * DEC : po * 128 + (p + 1) * DEC, :]))
                return acc * e + tgot[half, t, at, :].astype(FL)

            lax.fori_loop(0, rows, one, jnp.zeros((128, 128), FL))
        for i in range(1, rows):
            down(half, (row + i) % rows, row).start()
        crow[half, row] = cb[half, row]

    def scan_blocks(half):
        for i in range(1, rows):
            t = (row + i) % rows
            down(half, t, t).wait_recv()
        for k in range(gq):

            def one(i, _):
                p = k * PAIRS + i
                acc = crow[half, p // po, whole(p % po), :].astype(FL)
                for b in blocks(half):
                    back[half, b, whole(p), :] = acc.astype(BF)
                    acc = acc * es[b, p, 0:1] + got[half, b, whole(p), :].astype(FL)
                return 0

            lax.fori_loop(0, PAIRS, one, 0)
            for i in range(1, ROW):
                ret(half, k, (y + i) % ROW, y).start()
        cg[half, y] = back[half, y]

    row_totals(0)
    lax.fori_loop(share[0], share[1], local, 0)
    scan_rows(0)
    lax.fori_loop(share[1], share[2], local, 0)
    scan_blocks(0)
    row_totals(1)
    lax.fori_loop(share[2], share[3], local, 0)
    scan_rows(1)
    scan_blocks(1)

    def lane_cat(ref, half, t, k):
        return jnp.concatenate(
            [ref[half, t, pl.ds(pl.multiple_of((k * PAIRS + p) * 128, 128), 128), :] for p in range(PAIRS)], axis=1
        )

    def landed(half, k, t):
        @pl.when(t != y)
        def _():
            ret(half, k, t, t).wait_recv()

    def slices(g):
        return pl.ds(pl.multiple_of(g * GW, GW), GW), pl.ds(pl.multiple_of(g * NSTATE, NSTATE), NSTATE)

    def carried(j, _):
        k, t = j // ROW, (y + j) % ROW
        g = t * gq + k
        landed(0, k, t)
        lanes, glanes = slices(g)
        sel2 = sel_s[g]
        dyw = (dy_ref[:, lanes].astype(FL) * dot(ew_s[...], sel2)).astype(BF)
        car = lane_cat(cg, 0, t, k)
        r_acc[...] += gather_heads(dyw.astype(FL) * dot(r_ref[:, glanes], car), sel2[:heads])
        dr_ref[:, glanes] = (dri[:, glanes] + dot_nt(dyw, car)).astype(BF)
        return 0

    lax.fori_loop(0, groups, carried, 0)

    def returned(j, _):
        k, t = j // ROW, (y + j) % ROW
        g = t * gq + k
        landed(1, k, t)
        lanes, glanes = slices(g)
        sel2 = sel_s[g]
        sel = sel2[:heads]
        te = dot(te_s[...], sel2)
        xt = xt_s[:, lanes]
        ea = dot(full_s[...], sel2)[0:1]
        car, gst, own = lane_cat(cg, 0, t, k), lane_cat(cg, 1, t, k), lane_cat(sd, 0, t, k)
        zg = dot(w_ref[:, glanes], gst)
        c_acc[...] += gather_heads(xt.astype(FL) * zg, sel)
        ends = jnp.sum(gst.astype(FL) * (own.astype(FL) + ea * car.astype(FL)), axis=0, keepdims=True)
        dl_acc[...] += gather_heads(jnp.broadcast_to(ends, (8, GW)), sel)[0:1]
        dw_ref[:, glanes] = (dwi[:, glanes] + dot_nt(xt, gst)).astype(BF)
        xt_s[:, lanes] = (dxa[:, lanes] + te * zg).astype(BF)
        pltpu.make_async_copy(xt_s.at[:, lanes], dx_hbm.at[:, lanes], out_sem.at[g]).start()
        return 0

    lax.fori_loop(0, groups, returned, 0)
    rate = -jnp.exp(prm_s[1:2])
    trow = lax.broadcasted_iota(jnp.int32, (BLOCK, heads), 0)
    dwithin = r_acc[...] - c_acc[...] + jnp.where(trow == BLOCK - 1, dl_acc[...], 0.0)
    dld = tri_sum(triangle(True), dwithin)
    draw = (c_acc[...] / step_s[...] + rate * dld) * sig_s[...]
    sums = jnp.concatenate(
        [
            jnp.sum(dld * decay_s[...], axis=0, keepdims=True),
            jnp.sum(draw, axis=0, keepdims=True),
            sk_acc[...],
            jnp.zeros((5, heads), FL),
        ],
        axis=0,
    )
    dstep_ref[...] = draw.astype(BF)
    sums = total(sums, hy, at_cell, cell, in_cell, hy_s, hy_r)
    sums = total(sums, hr, row, rows, in_column, hr_s, hr_r) * factor
    hg_ref[...] = pltpu.roll(sums, lax.rem(heads - c * owned, heads), 1)
    for half in range(2):
        for i in range(1, ROW):
            for k in range(gq):
                out(half, k, (y + i) % ROW, y).wait_send()
                ret(half, k, (y + i) % ROW, y).wait_send()
        for i in range(1, rows):
            up(half, tb, (row + i) % rows, row).wait_send()
            down(half, (row + i) % rows, row).wait_send()

    def written(g, _):
        lanes = pl.ds(pl.multiple_of(g * GW, GW), GW)
        pltpu.make_async_copy(xt_s.at[:, lanes], dx_hbm.at[:, lanes], out_sem.at[g]).wait()
        return 0

    lax.fori_loop(0, groups, written, 0)


def finish(
    owned, dx_in, dw_in, dr_in, ds_in, hg_in, dx_out, dw_out, dr_out, ds_out, hg_out, dx, dw, dr, ds, hg, own, sem
):
    step = BLOCK // PARTS
    parts = [pl.ds(i * step, step) for i in range(PARTS)]
    moves = [(hg_in, hg, hg_out)] + [(dx_in.at[p], dx.at[p], dx_out.at[p]) for p in parts]
    moves += [(dw_in, dw, dw_out), (dr_in, dr, dr_out), (ds_in, ds, ds_out)]
    loads = [pltpu.make_async_copy(a, b, sem.at[0, i]) for i, (a, b, _) in enumerate(moves)]
    stores = [
        pltpu.make_async_copy(own if i == 0 else b, c, sem.at[1, i]) for i, (_, b, c) in enumerate(moves)
    ]
    for load in loads:
        load.start()
    for i, (load, store) in enumerate(zip(loads, stores)):
        load.wait()
        if i == 0:
            own[...] = hg[:3, :owned]
        store.start()
    for store in stores:
        store.wait()


def body(head_inputs, write_proj, read_projection, step_raw, output_grad, decay_log, step_bias, skip_gain):
    n, dps = lax.axis_size("seq"), lax.axis_size("dp")
    x, w, r, raw, dy = head_inputs[0], write_proj[0], read_projection[0], step_raw[0], output_grad[0]
    heads = raw.shape[1]
    groups = heads // PER_GROUP
    owned = heads // n
    factor = 1.0 / math.sqrt(dps * n * BLOCK * HEADDIM)
    vm = pl.BlockSpec(memory_space=pltpu.VMEM)
    sm = pl.BlockSpec(memory_space=pltpu.SMEM)
    hbm = pl.BlockSpec(memory_space=pl.ANY)
    cat2 = pltpu.VMEM((BLOCK, 2 * heads), BF)
    cat1 = pltpu.VMEM((HALF, 2 * heads), BF)
    full = pltpu.VMEM((BLOCK, heads), FL)
    tr = pltpu.VMEM((heads, BLOCK), FL)
    row = pltpu.VMEM((1, heads), FL)
    wide = pltpu.VMEM((BLOCK, GW), FL)
    rows, gq = n // ROW, groups // ROW
    pq = gq * PAIRS
    po = pq // rows

    def small(count):
        return pltpu.VMEM((count, 8, heads), FL)

    sem = pltpu.SemaphoreType.DMA
    dx, dw, dr, dstep, hg = pl.pallas_call(
        functools.partial(kernel, heads, groups, n, dps, factor),
        out_shape=[
            jax.ShapeDtypeStruct(x.shape, BF),
            jax.ShapeDtypeStruct(w.shape, BF),
            jax.ShapeDtypeStruct(r.shape, BF),
            jax.ShapeDtypeStruct(raw.shape, BF),
            jax.ShapeDtypeStruct((8, heads), FL),
        ],
        in_specs=[hbm] * 4 + [vm] + [sm] * 3,
        out_specs=[hbm] + [vm] * 4,
        scratch_shapes=[
            pltpu.VMEM(x.shape, BF), pltpu.VMEM(x.shape, BF), pltpu.VMEM(w.shape, BF), pltpu.VMEM(r.shape, BF),
            pltpu.VMEM((8, heads), FL), pltpu.VMEM((groups, 2 * heads, GW), BF), full, full, full,
            full, tr, tr, cat2, cat2, cat1, cat1,
            pltpu.VMEM((DEC, heads), BF), pltpu.VMEM((8, 2 * heads), BF),
            full, full, row, row,
            pltpu.VMEM(x.shape, FL), wide, wide, pltpu.VMEM(r.shape, FL), pltpu.VMEM(w.shape, FL), pltpu.VMEM(x.shape, BF),
            pltpu.VMEM((2, ROW, pq * 128 + pq * DEC, 128), BF), pltpu.VMEM((2, ROW, pq * 128 + pq * DEC, 128), BF),
            pltpu.VMEM((2, ROW, pq * 128, 128), BF), pltpu.VMEM((2, ROW, pq * 128, 128), BF),
            pltpu.VMEM((ROW, pq, 8, 128), FL),
            pltpu.VMEM((2, rows, po * (128 + DEC), 128), BF), pltpu.VMEM((2, rows, po * (128 + DEC), 128), BF),
            pltpu.VMEM((2, rows, po * 128, 128), BF), pltpu.VMEM((2, rows, po * 128, 128), BF),
            small(ROW), small(rows), small(ROW * dps), small(rows),
            sem((4,)), sem((groups,)), sem((2, gq, ROW)), sem((2, gq, ROW)), sem((2, gq, ROW)), sem((2, gq, ROW)),
            sem((2, rows)), sem((2, rows)), sem((2, rows)), sem((2, rows)),
            sem((ROW,)), sem((ROW,)), sem((rows,)), sem((rows,)),
            sem((ROW * dps,)), sem((ROW * dps,)), sem((rows,)), sem((rows,)),
        ],
        compiler_params=pltpu.CompilerParams(
            collective_id=0, has_side_effects=True, vmem_limit_bytes=60 * 2**20
        ),
        name="mixer_backward",
    )(x, dy, w, r, raw, step_bias, decay_log, skip_gain)
    dx, dw, dr, dstep, hg = pl.pallas_call(
        functools.partial(finish, owned),
        out_shape=[jax.ShapeDtypeStruct(a.shape, BF) for a in (dx, dw, dr, dstep)]
        + [jax.ShapeDtypeStruct((3, owned), FL)],
        in_specs=[hbm] * 5,
        out_specs=[hbm] * 5,
        scratch_shapes=[pltpu.VMEM(a.shape, BF) for a in (dx, dw, dr, dstep)]
        + [pltpu.VMEM(hg.shape, FL), pltpu.VMEM((3, owned), FL), sem((2, 4 + PARTS))],
        name="results",
    )(dx, dw, dr, dstep, hg)
    return (dx[None], dw[None], dr[None], dstep[None], hg)


def solution(mesh):
    tok = P("dp", "seq", None)
    return jax.shard_map(
        body,
        mesh=mesh,
        in_specs=(tok, tok, tok, tok, tok, P("seq"), P("seq"), P("seq")),
        out_specs=(tok, tok, tok, tok, P(None, "seq")),
        check_vma=False,
    )
```

```python
import functools
import math

import jax
import jax.numpy as jnp
from jax import lax
from jax.experimental import pallas as pl
from jax.experimental.pallas import tpu as pltpu
from jax.sharding import PartitionSpec as P

HEADDIM = 64
NSTATE = 128
BLOCK = 256
HALF = 128
PER_GROUP = 16
PAIRS = 8
GW = PER_GROUP * HEADDIM
ROW = 4
DEC = 16
PARTS = 4

BF = jnp.bfloat16
FL = jnp.float32
MESH = pl.DeviceIdType.MESH


def dot(a, b):
    return jnp.dot(a, b, preferred_element_type=FL)


def dot_nt(a, b):
    return lax.dot_general(a, b, (((1,), (1,)), ((), ())), preferred_element_type=FL)


def dot_tn(a, b):
    return lax.dot_general(a, b, (((0,), (0,)), ((), ())), preferred_element_type=FL)


def hi_lo(a):
    hi = a.astype(BF)
    return hi, (a - hi.astype(FL)).astype(BF)


def three(a):
    hi, _ = hi_lo(a)
    rest = a - hi.astype(FL)
    mid, low = hi_lo(rest)
    return hi, mid, low


def cat_hi_lo(a):
    return jnp.concatenate(hi_lo(a), axis=1)


def tri_sum(tri, a):
    hi, mid, low = three(a)
    return dot(tri, hi) + dot(tri, mid) + dot(tri, low)


def triangle(upper):
    row = lax.broadcasted_iota(jnp.int32, (BLOCK, BLOCK), 0)
    col = lax.broadcasted_iota(jnp.int32, (BLOCK, BLOCK), 1)
    keep = (col >= row) if upper else (col <= row)
    return jnp.where(keep, 1.0, 0.0).astype(BF)


def spread(g, heads):
    row = lax.broadcasted_iota(jnp.int32, (heads, GW), 0)
    col = lax.broadcasted_iota(jnp.int32, (heads, GW), 1)
    return jnp.where(row == g * PER_GROUP + col // HEADDIM, 1.0, 0.0).astype(BF)


def gather_heads(p, sel):
    hi, lo = hi_lo(p)
    return dot_nt(hi, sel) + dot_nt(lo, sel)


def rates(raw, prm):
    v = raw.astype(FL) + prm[0:1]
    e = jnp.exp(-jnp.abs(v))
    small = e * (1.0 - e * (0.5 - e * (1.0 / 3 - e * (0.25 - e * 0.2))))
    step = jnp.maximum(v, 0.0) + jnp.where(e < 0.03125, small, jnp.log(1.0 + e))
    rate = -jnp.exp(prm[1:2])
    decay = rate * step
    within = tri_sum(triangle(False), decay)
    return v, step, rate, decay, within


def last_terms(last):
    h, m, l = three(last)
    return jnp.concatenate([h, m, l, jnp.zeros((DEC - 3, last.shape[1]), BF)], axis=0)


def half_states(g, rows_ref, cat, proj_ref, sel2, out_ref, at, keep):
    lanes = pl.ds(pl.multiple_of(g * GW, GW), GW)
    glanes = pl.ds(pl.multiple_of(g * NSTATE, NSTATE), NSTATE)
    scaled = (rows_ref[:, lanes].astype(FL) * dot(cat, sel2)).astype(BF)
    if keep is not None:
        keep[:, lanes] = scaled
    state = dot_tn(proj_ref[:, glanes], scaled).astype(BF)
    for p in range(PAIRS):
        out_ref[at + (pl.ds(p * 128, 128),)] = state[:, p * 128 : p * 128 + 128]


def intra(g, heads, x_ref, dy_ref, w_ref, r_ref, within, wt_s, st_s, cat_tm, cat_fm, dxa, pr, pc, sel2):
    lanes = pl.ds(pl.multiple_of(g * GW, GW), GW)
    glanes = pl.ds(pl.multiple_of(g * NSTATE, NSTATE), NSTATE)
    wg, rg = w_ref[:, glanes], r_ref[:, glanes]
    row = lax.broadcasted_iota(jnp.int32, (HALF, HALF), 0)
    col = lax.broadcasted_iota(jnp.int32, (HALF, HALF), 1)
    lower = col <= row
    first = lax.broadcasted_iota(jnp.int32, (HALF, 128), 1) < HEADDIM
    scores = dot_nt(rg, wg)
    tm = dot(cat_tm, sel2)
    x0 = x_ref[:HALF, lanes].astype(FL)
    xt1 = (x0 * tm).astype(BF)
    dy1 = (dy_ref[HALF:, lanes].astype(FL) * dot(cat_fm, sel2)).astype(BF)
    sb = scores[HALF:, :HALF].astype(BF)
    z = dot(sb, xt1)
    yb = dot_tn(sb, dy1)
    ds_low = dot_nt(dy1, xt1)
    pr[:HALF, :] = jnp.zeros((HALF, GW), FL)
    pr[HALF:, :] = dy1.astype(FL) * z
    pc[:HALF, :] = xt1.astype(FL) * yb
    pc[HALF:, :] = jnp.zeros((HALF, GW), FL)
    dxa[:HALF, lanes] = tm * yb
    dxa[HALF:, lanes] = jnp.zeros((HALF, GW), FL)
    wr = pltpu.roll(within, lax.rem(heads - g * PER_GROUP, heads), 1)
    wt = wt_s[pl.ds(pl.multiple_of(g * PER_GROUP, PER_GROUP), PER_GROUP), :]
    st = st_s[pl.ds(pl.multiple_of(g * PER_GROUP, PER_GROUP), PER_GROUP), :]
    ds_diag = []
    for sub in range(2):
        rs = slice(sub * HALF, sub * HALF + HALF)
        sd = jnp.where(lower, scores[rs, rs], 0.0)
        ds = jnp.zeros((HALF, HALF), FL)
        for p in range(PAIRS):
            pls = pl.ds(pl.multiple_of(g * GW + p * 128, 128), 128)
            here = slice(p * 128, p * 128 + 128)
            xp, dyp = x_ref[rs, pls], dy_ref[rs, pls]
            none = jnp.zeros_like(xp)
            xst = jnp.concatenate([jnp.where(first, xp, none), jnp.where(first, none, xp)], axis=0)
            dyst = jnp.concatenate([jnp.where(first, dyp, none), jnp.where(first, none, dyp)], axis=0)
            dw = dot_nt(dyp, xst)
            parts = []
            for k in range(2):
                h = 2 * p + k
                gap = jnp.minimum(wr[rs, h : h + 1] - wt[h : h + 1, rs], 0.0)
                es = jnp.exp(gap) * st[h : h + 1, rs]
                ds += dw[:, k * HALF : k * HALF + HALF] * es
                parts.append((sd * es).astype(BF))
            y = dot(jnp.concatenate(parts, axis=1), xst)
            dxp = dot_tn(jnp.concatenate(parts, axis=0), dyst)
            pr[rs, here] += dyp.astype(FL) * y
            pc[rs, here] += xp.astype(FL) * dxp
            dxa[rs, pls] += dxp
        ds_diag.append(jnp.where(lower, ds, 0.0))
    top = jnp.concatenate([ds_diag[0], jnp.zeros((HALF, HALF), FL)], axis=1)
    low = jnp.concatenate([ds_low, ds_diag[1]], axis=1)
    dscore = jnp.concatenate([top, low], axis=0).astype(BF)
    return dot(dscore, wg), dot_tn(dscore, rg)


def kernel(
    heads, groups, n, dps, factor,
    x_hbm, dy_hbm, w_hbm, r_hbm, raw_ref, bias_ref, dlog_ref, gain_ref,
    dx_hbm, dw_hbm, dr_hbm, ds_hbm, hg_ref,
    dw_ref, dr_ref, dstep_ref, x_ref, dy_ref, w_ref, r_ref, prm_s, sel_s, step_s, decay_s, sig_s, within_s, wt_s, st_s, te_s, ew_s, tm_s, fm_s, l3_s, full_s,
    r_acc, c_acc, dl_acc, sk_acc, dxa, pr, pc, dri, dwi, xt_s,
    sd, got, back, cg, es, tb, tgot, cb, crow, py, pr_all, hy, hr,
    in_sem, out_sem, end_sem, s1, r1, s2, r2, s3, r3, s4, r4, py_s, py_r, pz_s, pz_r, hy_s, hy_r, hr_s, hr_r,
):
    c = lax.axis_index("seq")
    d = lax.axis_index("dp")
    loads = [
        pltpu.make_async_copy(a, b, in_sem.at[i])
        for i, (a, b) in enumerate(((x_hbm, x_ref), (dy_hbm, dy_ref), (w_hbm, w_ref), (r_hbm, r_ref)))
    ]
    for load in loads:
        load.start()

    y, row, rows = c % ROW, c // ROW, n // ROW
    gq = groups // ROW
    pq = gq * PAIRS
    po = pq // rows

    def in_row(t):
        return {"seq": row * ROW + t}

    def in_column(t):
        return {"seq": t * ROW + y}

    def in_cell(t):
        return {"seq": row * ROW + t // dps, "dp": t % dps}

    barrier = pltpu.get_barrier_semaphore()
    for i in range(1, rows):
        pl.semaphore_signal(barrier, inc=1, device_id=in_column((row + i) % rows), device_id_type=MESH)
    cell, at_cell = ROW * dps, y * dps + d
    for i in range(1, cell):
        pl.semaphore_signal(barrier, inc=1, device_id=in_cell((at_cell + i) % cell), device_id_type=MESH)
    for g in range(groups):
        one = spread(g, heads)
        sel_s[g, :heads] = one
        sel_s[g, heads:] = one
    for acc in (r_acc, c_acc, dl_acc, sk_acc):
        acc[...] = jnp.zeros_like(acc)
    pl.semaphore_wait(barrier, rows - 1 + cell - 1)

    lane = lax.broadcasted_iota(jnp.int32, (8, heads), 1)
    which = lax.broadcasted_iota(jnp.int32, (8, heads), 0)
    mine = jnp.zeros((8, heads), FL)
    owned = heads // n
    for i, ref in enumerate((bias_ref, dlog_ref, gain_ref)):
        for k in range(owned):
            mine = jnp.where((which == i) & (lane == c * owned + k), ref[k], mine)

    def total(value, buf, me, count, where, send, recv):
        buf[me] = value

        def copy(i, slot):
            return pltpu.make_async_remote_copy(
                src_ref=buf.at[slot], dst_ref=buf.at[slot], send_sem=send.at[i], recv_sem=recv.at[slot],
                device_id=where((me + i) % count), device_id_type=MESH,
            )

        for i in range(1, count):
            copy(i, me).start()
        for i in range(1, count):
            copy(i, me).wait_send()
            copy(i, (me + i) % count).wait_recv()
        return jnp.sum(buf[...], axis=0)

    mine = total(mine, py, y, ROW, in_row, py_s, py_r)
    prm_s[...] = total(mine, pr_all, row, rows, in_column, pz_s, pz_r)
    v, step, _, decay, within = rates(raw_ref[...], prm_s[...])
    within_s[...] = within
    step_s[...] = step
    decay_s[...] = decay
    sig_s[...] = 1.0 / (1.0 + jnp.exp(-v))
    last = within[BLOCK - 1 : BLOCK]
    te_s[...] = cat_hi_lo(jnp.exp(last - within) * step)
    ew_s[...] = cat_hi_lo(jnp.exp(within))
    l3_s[...] = last_terms(last)

    def rest():
        within, step = within_s[...], step_s[...]
        last, mid = within[BLOCK - 1 : BLOCK], within[HALF - 1 : HALF]
        wt_s[...] = within.T
        st_s[...] = step.T
        tm_s[...] = cat_hi_lo(jnp.exp(mid - within[:HALF]) * step[:HALF])
        fm_s[...] = cat_hi_lo(jnp.exp(within[HALF:] - mid))
        full_s[...] = cat_hi_lo(jnp.concatenate([jnp.exp(last), prm_s[2:3], jnp.zeros((6, heads), FL)], axis=0))

    for load in loads:
        load.wait()

    def span(half, k):
        return pl.ds(k * PAIRS * 128, PAIRS * 128 + (pq * DEC if half == 0 and k == gq - 1 else 0))

    def out(half, k, t, slot):
        at = span(half, k)
        return pltpu.make_async_remote_copy(
            src_ref=sd.at[half, t, at], dst_ref=got.at[half, slot, at],
            send_sem=s1.at[half, k, t], recv_sem=r1.at[half, k, slot], device_id=in_row(t), device_id_type=MESH,
        )

    def make(half, t, k):
        g = t * gq + k
        at = (half, t)
        src = (x_ref, te_s, w_ref) if half == 0 else (dy_ref, ew_s, r_ref)
        half_states(g, src[0], src[1][...], src[2], sel_s[g], sd.at[half, t, pl.ds(k * PAIRS * 128, PAIRS * 128)], (), xt_s if half == 0 else None)
        if half == 0:
            lx = dot(l3_s[...], sel_s[g, :heads]).astype(BF)
            for p in range(PAIRS):
                at = pq * 128 + (k * PAIRS + p) * DEC
                sd[0, t, at : at + DEC, :] = lx[:, p * 128 : p * 128 + 128]

    for half in range(2):
        for k in range(gq):

            def send(i, _):
                t = (y + i) % ROW
                make(half, t, k)
                out(half, k, t, y).start()
                return 0

            lax.fori_loop(1, ROW, send, 0)
        for k in range(gq):
            make(half, y, k)
        got[half, y] = sd[half, y]

    def local(g, _):
        glanes = pl.ds(pl.multiple_of(g * NSTATE, NSTATE), NSTATE)
        sel2 = sel_s[g]
        dr_i, dw_i = intra(
            g, heads, x_ref, dy_ref, w_ref, r_ref, within_s[...], wt_s, st_s, tm_s[...], fm_s[...], dxa, pr, pc, sel2
        )
        lanes = pl.ds(pl.multiple_of(g * GW, GW), GW)
        dyf = dy_ref[:, lanes].astype(FL)
        dxa[:, lanes] += dot(full_s[...], sel2)[1:2] * dyf
        skips = jnp.sum(x_ref[:, lanes].astype(FL) * dyf, axis=0, keepdims=True)
        sk_acc[...] += gather_heads(jnp.broadcast_to(skips, (8, GW)), sel2[:heads])[0:1]
        dri[:, glanes] = dr_i
        dwi[:, glanes] = dw_i
        r_acc[...] += gather_heads(pr[...], sel2[:heads])
        c_acc[...] += gather_heads(pc[...], sel2[:heads])
        return 0

    rest()
    share = (groups * 5 // 8, groups * 6 // 8, groups * 7 // 8, groups)
    lax.fori_loop(0, share[0], local, 0)

    def arrived(half):
        for k in range(gq):
            for i in range(1, ROW):
                t = (y + i) % ROW
                out(half, k, t, t).wait_recv()

    def whole(p):
        return pl.ds(pl.multiple_of(p * 128, 128), 128)

    def up(half, src, t, slot):
        at = pl.ds(0, po * 128 + (po * DEC if half == 0 else 0))
        return pltpu.make_async_remote_copy(
            src_ref=src.at[half, t, at], dst_ref=tgot.at[half, slot, at],
            send_sem=s3.at[half, t], recv_sem=r3.at[half, slot], device_id=in_column(t), device_id_type=MESH,
        )

    def down(half, t, slot):
        return pltpu.make_async_remote_copy(
            src_ref=cb.at[half, t], dst_ref=crow.at[half, slot],
            send_sem=s4.at[half, t], recv_sem=r4.at[half, slot], device_id=in_column(t), device_id_type=MESH,
        )

    def ret(half, k, t, slot):
        at = pl.ds(pl.multiple_of(k * (PAIRS * 128), PAIRS * 128), PAIRS * 128)
        return pltpu.make_async_remote_copy(
            src_ref=back.at[half, t, at], dst_ref=cg.at[half, slot, at],
            send_sem=s2.at[half, k, t], recv_sem=r2.at[half, k, slot], device_id=in_row(t), device_id_type=MESH,
        )

    def blocks(half):
        return range(ROW) if half == 0 else range(ROW - 1, -1, -1)

    def log_decay(rows3):
        f = rows3.astype(FL)
        return f[0:1] + f[1:2] + f[2:3]

    def row_totals(half):
        arrived(half)

        def one(p, _):
            if half == 0:
                logs = jnp.zeros((1, 128), FL)
                for b in range(ROW):
                    log = log_decay(got[0, b, pl.ds(pl.multiple_of(pq * 128 + p * DEC, DEC), DEC), :])
                    es[b, p] = jnp.broadcast_to(jnp.exp(log), (8, 128))
                    logs += log
                h, m, l = three(logs)
                terms = jnp.concatenate([h, m, l, jnp.zeros((DEC - 3, 128), BF)], axis=0)
                tb[0, p // po, pl.ds(pl.multiple_of(po * 128 + (p % po) * DEC, DEC), DEC), :] = terms
            acc = jnp.zeros((128, 128), FL)
            for b in blocks(half):
                acc = acc * es[b, p, 0:1] + got[half, b, whole(p), :].astype(FL)
            tb[half, p // po, whole(p % po), :] = acc.astype(BF)
            return 0

        lax.fori_loop(0, pq, one, 0)
        for i in range(1, rows):
            up(half, tb, (row + i) % rows, row).start()
        tgot[half, row] = tb[half, row]

    def scan_rows(half):
        for i in range(1, rows):
            t = (row + i) % rows
            up(half, tb, t, t).wait_recv()
        for p in range(po):
            at = slice(p * 128, p * 128 + 128)

            def one(i, acc):
                t = i if half == 0 else rows - 1 - i
                cb[half, t, at, :] = acc.astype(BF)
                e = jnp.exp(log_decay(tgot[0, t, po * 128 + p * DEC : po * 128 + (p + 1) * DEC, :]))
                return acc * e + tgot[half, t, at, :].astype(FL)

            lax.fori_loop(0, rows, one, jnp.zeros((128, 128), FL))
        for i in range(1, rows):
            down(half, (row + i) % rows, row).start()
        crow[half, row] = cb[half, row]

    def scan_blocks(half):
        for i in range(1, rows):
            t = (row + i) % rows
            down(half, t, t).wait_recv()
        for k in range(gq):

            def one(i, _):
                p = k * PAIRS + i
                acc = crow[half, p // po, whole(p % po), :].astype(FL)
                for b in blocks(half):
                    back[half, b, whole(p), :] = acc.astype(BF)
                    acc = acc * es[b, p, 0:1] + got[half, b, whole(p), :].astype(FL)
                return 0

            lax.fori_loop(0, PAIRS, one, 0)
            for i in range(1, ROW):
                ret(half, k, (y + i) % ROW, y).start()
        cg[half, y] = back[half, y]

    row_totals(0)
    lax.fori_loop(share[0], share[1], local, 0)
    scan_rows(0)
    lax.fori_loop(share[1], share[2], local, 0)
    scan_blocks(0)
    row_totals(1)
    lax.fori_loop(share[2], share[3], local, 0)
    scan_rows(1)
    scan_blocks(1)

    def lane_cat(ref, half, t, k):
        return jnp.concatenate(
            [ref[half, t, pl.ds(pl.multiple_of((k * PAIRS + p) * 128, 128), 128), :] for p in range(PAIRS)], axis=1
        )

    def landed(half, k, t):
        @pl.when(t != y)
        def _():
            ret(half, k, t, t).wait_recv()

    def slices(g):
        return pl.ds(pl.multiple_of(g * GW, GW), GW), pl.ds(pl.multiple_of(g * NSTATE, NSTATE), NSTATE)

    def carried(j, _):
        k, t = j // ROW, (y + j) % ROW
        g = t * gq + k
        landed(0, k, t)
        lanes, glanes = slices(g)
        sel2 = sel_s[g]
        dyw = (dy_ref[:, lanes].astype(FL) * dot(ew_s[...], sel2)).astype(BF)
        car = lane_cat(cg, 0, t, k)
        r_acc[...] += gather_heads(dyw.astype(FL) * dot(r_ref[:, glanes], car), sel2[:heads])
        dr_ref[:, glanes] = (dri[:, glanes] + dot_nt(dyw, car)).astype(BF)
        return 0

    lax.fori_loop(0, groups, carried, 0)
    ends = [
        pltpu.make_async_copy(a, b, end_sem.at[i])
        for i, (a, b) in enumerate(((dr_ref, dr_hbm), (dw_ref, dw_hbm), (dstep_ref, ds_hbm)))
    ]
    ends[0].start()

    def returned(j, _):
        k, t = j // ROW, (y + j) % ROW
        g = t * gq + k
        landed(1, k, t)
        lanes, glanes = slices(g)
        sel2 = sel_s[g]
        sel = sel2[:heads]
        te = dot(te_s[...], sel2)
        xt = xt_s[:, lanes]
        ea = dot(full_s[...], sel2)[0:1]
        car, gst, own = lane_cat(cg, 0, t, k), lane_cat(cg, 1, t, k), lane_cat(sd, 0, t, k)
        zg = dot(w_ref[:, glanes], gst)
        c_acc[...] += gather_heads(xt.astype(FL) * zg, sel)
        ends = jnp.sum(gst.astype(FL) * (own.astype(FL) + ea * car.astype(FL)), axis=0, keepdims=True)
        dl_acc[...] += gather_heads(jnp.broadcast_to(ends, (8, GW)), sel)[0:1]
        dw_ref[:, glanes] = (dwi[:, glanes] + dot_nt(xt, gst)).astype(BF)
        xt_s[:, lanes] = (dxa[:, lanes] + te * zg).astype(BF)
        pltpu.make_async_copy(xt_s.at[:, lanes], dx_hbm.at[:, lanes], out_sem.at[g]).start()
        return 0

    lax.fori_loop(0, groups, returned, 0)
    ends[1].start()
    rate = -jnp.exp(prm_s[1:2])
    trow = lax.broadcasted_iota(jnp.int32, (BLOCK, heads), 0)
    dwithin = r_acc[...] - c_acc[...] + jnp.where(trow == BLOCK - 1, dl_acc[...], 0.0)
    dld = tri_sum(triangle(True), dwithin)
    draw = (c_acc[...] / step_s[...] + rate * dld) * sig_s[...]
    sums = jnp.concatenate(
        [
            jnp.sum(dld * decay_s[...], axis=0, keepdims=True),
            jnp.sum(draw, axis=0, keepdims=True),
            sk_acc[...],
            jnp.zeros((5, heads), FL),
        ],
        axis=0,
    )
    dstep_ref[...] = draw.astype(BF)
    ends[2].start()
    sums = total(sums, hy, at_cell, cell, in_cell, hy_s, hy_r)
    sums = total(sums, hr, row, rows, in_column, hr_s, hr_r) * factor
    hg_ref[...] = pltpu.roll(sums, lax.rem(heads - c * owned, heads), 1)
    for half in range(2):
        for i in range(1, ROW):
            for k in range(gq):
                out(half, k, (y + i) % ROW, y).wait_send()
                ret(half, k, (y + i) % ROW, y).wait_send()
        for i in range(1, rows):
            up(half, tb, (row + i) % rows, row).wait_send()
            down(half, (row + i) % rows, row).wait_send()

    def written(g, _):
        lanes = pl.ds(pl.multiple_of(g * GW, GW), GW)
        pltpu.make_async_copy(xt_s.at[:, lanes], dx_hbm.at[:, lanes], out_sem.at[g]).wait()
        return 0

    lax.fori_loop(0, groups, written, 0)
    for end in ends:
        end.wait()


def finish(
    owned, dx_in, dw_in, dr_in, ds_in, hg_in, dx_out, dw_out, dr_out, ds_out, hg_out, dx, dw, dr, ds, hg, own, sem
):
    step = BLOCK // PARTS
    parts = [pl.ds(i * step, step) for i in range(PARTS)]
    moves = [(hg_in, hg, hg_out)] + [(dx_in.at[p], dx.at[p], dx_out.at[p]) for p in parts]
    moves += [(dw_in, dw, dw_out), (dr_in, dr, dr_out), (ds_in, ds, ds_out)]
    loads = [pltpu.make_async_copy(a, b, sem.at[0, i]) for i, (a, b, _) in enumerate(moves)]
    stores = [
        pltpu.make_async_copy(own if i == 0 else b, c, sem.at[1, i]) for i, (_, b, c) in enumerate(moves)
    ]
    for load in loads:
        load.start()
    for i, (load, store) in enumerate(zip(loads, stores)):
        load.wait()
        if i == 0:
            own[...] = hg[:3, :owned]
        store.start()
    for store in stores:
        store.wait()


def body(head_inputs, write_proj, read_projection, step_raw, output_grad, decay_log, step_bias, skip_gain):
    n, dps = lax.axis_size("seq"), lax.axis_size("dp")
    x, w, r, raw, dy = head_inputs[0], write_proj[0], read_projection[0], step_raw[0], output_grad[0]
    heads = raw.shape[1]
    groups = heads // PER_GROUP
    owned = heads // n
    factor = 1.0 / math.sqrt(dps * n * BLOCK * HEADDIM)
    vm = pl.BlockSpec(memory_space=pltpu.VMEM)
    sm = pl.BlockSpec(memory_space=pltpu.SMEM)
    hbm = pl.BlockSpec(memory_space=pl.ANY)
    cat2 = pltpu.VMEM((BLOCK, 2 * heads), BF)
    cat1 = pltpu.VMEM((HALF, 2 * heads), BF)
    full = pltpu.VMEM((BLOCK, heads), FL)
    tr = pltpu.VMEM((heads, BLOCK), FL)
    row = pltpu.VMEM((1, heads), FL)
    wide = pltpu.VMEM((BLOCK, GW), FL)
    rows, gq = n // ROW, groups // ROW
    pq = gq * PAIRS
    po = pq // rows

    def small(count):
        return pltpu.VMEM((count, 8, heads), FL)

    sem = pltpu.SemaphoreType.DMA
    dx, dw, dr, dstep, hg = pl.pallas_call(
        functools.partial(kernel, heads, groups, n, dps, factor),
        out_shape=[
            jax.ShapeDtypeStruct(x.shape, BF),
            jax.ShapeDtypeStruct(w.shape, BF),
            jax.ShapeDtypeStruct(r.shape, BF),
            jax.ShapeDtypeStruct(raw.shape, BF),
            jax.ShapeDtypeStruct((8, heads), FL),
        ],
        in_specs=[hbm] * 4 + [vm] + [sm] * 3,
        out_specs=[hbm] * 4 + [vm],
        scratch_shapes=[
            pltpu.VMEM(w.shape, BF), pltpu.VMEM(r.shape, BF), pltpu.VMEM(raw.shape, BF),
            pltpu.VMEM(x.shape, BF), pltpu.VMEM(x.shape, BF), pltpu.VMEM(w.shape, BF), pltpu.VMEM(r.shape, BF),
            pltpu.VMEM((8, heads), FL), pltpu.VMEM((groups, 2 * heads, GW), BF), full, full, full,
            full, tr, tr, cat2, cat2, cat1, cat1,
            pltpu.VMEM((DEC, heads), BF), pltpu.VMEM((8, 2 * heads), BF),
            full, full, row, row,
            pltpu.VMEM(x.shape, FL), wide, wide, pltpu.VMEM(r.shape, FL), pltpu.VMEM(w.shape, FL), pltpu.VMEM(x.shape, BF),
            pltpu.VMEM((2, ROW, pq * 128 + pq * DEC, 128), BF), pltpu.VMEM((2, ROW, pq * 128 + pq * DEC, 128), BF),
            pltpu.VMEM((2, ROW, pq * 128, 128), BF), pltpu.VMEM((2, ROW, pq * 128, 128), BF),
            pltpu.VMEM((ROW, pq, 8, 128), FL),
            pltpu.VMEM((2, rows, po * (128 + DEC), 128), BF), pltpu.VMEM((2, rows, po * (128 + DEC), 128), BF),
            pltpu.VMEM((2, rows, po * 128, 128), BF), pltpu.VMEM((2, rows, po * 128, 128), BF),
            small(ROW), small(rows), small(ROW * dps), small(rows),
            sem((4,)), sem((groups,)), sem((3,)), sem((2, gq, ROW)), sem((2, gq, ROW)), sem((2, gq, ROW)), sem((2, gq, ROW)),
            sem((2, rows)), sem((2, rows)), sem((2, rows)), sem((2, rows)),
            sem((ROW,)), sem((ROW,)), sem((rows,)), sem((rows,)),
            sem((ROW * dps,)), sem((ROW * dps,)), sem((rows,)), sem((rows,)),
        ],
        compiler_params=pltpu.CompilerParams(
            collective_id=0, has_side_effects=True, vmem_limit_bytes=60 * 2**20
        ),
        name="mixer_backward",
    )(x, dy, w, r, raw, step_bias, decay_log, skip_gain)
    dx, dw, dr, dstep, hg = pl.pallas_call(
        functools.partial(finish, owned),
        out_shape=[jax.ShapeDtypeStruct(a.shape, BF) for a in (dx, dw, dr, dstep)]
        + [jax.ShapeDtypeStruct((3, owned), FL)],
        in_specs=[hbm] * 5,
        out_specs=[hbm] * 5,
        scratch_shapes=[pltpu.VMEM(a.shape, BF) for a in (dx, dw, dr, dstep)]
        + [pltpu.VMEM(hg.shape, FL), pltpu.VMEM((3, owned), FL), sem((2, 4 + PARTS))],
        name="results",
    )(dx, dw, dr, dstep, hg)
    return (dx[None], dw[None], dr[None], dstep[None], hg)


def solution(mesh):
    tok = P("dp", "seq", None)
    return jax.shard_map(
        body,
        mesh=mesh,
        in_specs=(tok, tok, tok, tok, tok, P("seq"), P("seq"), P("seq")),
        out_specs=(tok, tok, tok, tok, P(None, "seq")),
        check_vma=False,
    )
```

```python
import functools
import math

import jax
import jax.numpy as jnp
from jax import lax
from jax.experimental import pallas as pl
from jax.experimental.pallas import tpu as pltpu
from jax.sharding import PartitionSpec as P

HEADDIM = 64
NSTATE = 128
BLOCK = 256
HALF = 128
PER_GROUP = 16
PAIRS = 8
GW = PER_GROUP * HEADDIM
ROW = 4
DEC = 16
PARTS = 4

BF = jnp.bfloat16
FL = jnp.float32
MESH = pl.DeviceIdType.MESH


def dot(a, b):
    return jnp.dot(a, b, preferred_element_type=FL)


def dot_nt(a, b):
    return lax.dot_general(a, b, (((1,), (1,)), ((), ())), preferred_element_type=FL)


def dot_tn(a, b):
    return lax.dot_general(a, b, (((0,), (0,)), ((), ())), preferred_element_type=FL)


def hi_lo(a):
    hi = a.astype(BF)
    return hi, (a - hi.astype(FL)).astype(BF)


def three(a):
    hi, _ = hi_lo(a)
    rest = a - hi.astype(FL)
    mid, low = hi_lo(rest)
    return hi, mid, low


def cat_hi_lo(a):
    return jnp.concatenate(hi_lo(a), axis=1)


def tri_sum(tri, a):
    hi, mid, low = three(a)
    return dot(tri, hi) + dot(tri, mid) + dot(tri, low)


def triangle(upper):
    row = lax.broadcasted_iota(jnp.int32, (BLOCK, BLOCK), 0)
    col = lax.broadcasted_iota(jnp.int32, (BLOCK, BLOCK), 1)
    keep = (col >= row) if upper else (col <= row)
    return jnp.where(keep, 1.0, 0.0).astype(BF)


def spread(g, heads):
    row = lax.broadcasted_iota(jnp.int32, (heads, GW), 0)
    col = lax.broadcasted_iota(jnp.int32, (heads, GW), 1)
    return jnp.where(row == g * PER_GROUP + col // HEADDIM, 1.0, 0.0).astype(BF)


def gather_heads(p, sel):
    hi, lo = hi_lo(p)
    return dot_nt(hi, sel) + dot_nt(lo, sel)


def rates(raw, prm):
    v = raw.astype(FL) + prm[0:1]
    e = jnp.exp(-jnp.abs(v))
    small = e * (1.0 - e * (0.5 - e * (1.0 / 3 - e * (0.25 - e * 0.2))))
    step = jnp.maximum(v, 0.0) + jnp.where(e < 0.03125, small, jnp.log(1.0 + e))
    rate = -jnp.exp(prm[1:2])
    decay = rate * step
    within = tri_sum(triangle(False), decay)
    return v, step, rate, decay, within


def last_terms(last):
    h, m, l = three(last)
    return jnp.concatenate([h, m, l, jnp.zeros((DEC - 3, last.shape[1]), BF)], axis=0)


def half_states(g, rows_ref, cat, proj_ref, sel2, out_ref, at, keep):
    lanes = pl.ds(pl.multiple_of(g * GW, GW), GW)
    glanes = pl.ds(pl.multiple_of(g * NSTATE, NSTATE), NSTATE)
    scaled = (rows_ref[:, lanes].astype(FL) * dot(cat, sel2)).astype(BF)
    if keep is not None:
        keep[:, lanes] = scaled
    state = dot_tn(proj_ref[:, glanes], scaled).astype(BF)
    for p in range(PAIRS):
        out_ref[at + (pl.ds(p * 128, 128),)] = state[:, p * 128 : p * 128 + 128]


def intra(g, heads, x_ref, dy_ref, w_ref, r_ref, within, wt_s, st_s, cat_tm, cat_fm, dxa, pr, pc, sel2):
    lanes = pl.ds(pl.multiple_of(g * GW, GW), GW)
    glanes = pl.ds(pl.multiple_of(g * NSTATE, NSTATE), NSTATE)
    wg, rg = w_ref[:, glanes], r_ref[:, glanes]
    row = lax.broadcasted_iota(jnp.int32, (HALF, HALF), 0)
    col = lax.broadcasted_iota(jnp.int32, (HALF, HALF), 1)
    lower = col <= row
    first = lax.broadcasted_iota(jnp.int32, (HALF, 128), 1) < HEADDIM
    scores = dot_nt(rg, wg)
    tm = dot(cat_tm, sel2)
    x0 = x_ref[:HALF, lanes].astype(FL)
    xt1 = (x0 * tm).astype(BF)
    dy1 = (dy_ref[HALF:, lanes].astype(FL) * dot(cat_fm, sel2)).astype(BF)
    sb = scores[HALF:, :HALF].astype(BF)
    z = dot(sb, xt1)
    yb = dot_tn(sb, dy1)
    ds_low = dot_nt(dy1, xt1)
    pr[:HALF, :] = jnp.zeros((HALF, GW), FL)
    pr[HALF:, :] = dy1.astype(FL) * z
    pc[:HALF, :] = xt1.astype(FL) * yb
    pc[HALF:, :] = jnp.zeros((HALF, GW), FL)
    dxa[:HALF, lanes] = tm * yb
    dxa[HALF:, lanes] = jnp.zeros((HALF, GW), FL)
    wr = pltpu.roll(within, lax.rem(heads - g * PER_GROUP, heads), 1)
    wt = wt_s[pl.ds(pl.multiple_of(g * PER_GROUP, PER_GROUP), PER_GROUP), :]
    st = st_s[pl.ds(pl.multiple_of(g * PER_GROUP, PER_GROUP), PER_GROUP), :]
    ds_diag = []
    for sub in range(2):
        rs = slice(sub * HALF, sub * HALF + HALF)
        sd = jnp.where(lower, scores[rs, rs], 0.0)
        ds = jnp.zeros((HALF, HALF), FL)
        for p in range(PAIRS):
            pls = pl.ds(pl.multiple_of(g * GW + p * 128, 128), 128)
            here = slice(p * 128, p * 128 + 128)
            xp, dyp = x_ref[rs, pls], dy_ref[rs, pls]
            none = jnp.zeros_like(xp)
            xst = jnp.concatenate([jnp.where(first, xp, none), jnp.where(first, none, xp)], axis=0)
            dyst = jnp.concatenate([jnp.where(first, dyp, none), jnp.where(first, none, dyp)], axis=0)
            dw = dot_nt(dyp, xst)
            parts = []
            for k in range(2):
                h = 2 * p + k
                gap = jnp.minimum(wr[rs, h : h + 1] - wt[h : h + 1, rs], 0.0)
                es = jnp.exp(gap) * st[h : h + 1, rs]
                ds += dw[:, k * HALF : k * HALF + HALF] * es
                parts.append((sd * es).astype(BF))
            y = dot(jnp.concatenate(parts, axis=1), xst)
            dxp = dot_tn(jnp.concatenate(parts, axis=0), dyst)
            pr[rs, here] += dyp.astype(FL) * y
            pc[rs, here] += xp.astype(FL) * dxp
            dxa[rs, pls] += dxp
        ds_diag.append(jnp.where(lower, ds, 0.0))
    top = jnp.concatenate([ds_diag[0], jnp.zeros((HALF, HALF), FL)], axis=1)
    low = jnp.concatenate([ds_low, ds_diag[1]], axis=1)
    dscore = jnp.concatenate([top, low], axis=0).astype(BF)
    return dot(dscore, wg), dot_tn(dscore, rg)


def kernel(
    heads, groups, n, dps, factor,
    x_hbm, dy_hbm, w_hbm, r_hbm, raw_ref, bias_ref, dlog_ref, gain_ref,
    dx_hbm, dw_hbm, dr_hbm, ds_hbm, hg_ref,
    dw_ref, dr_ref, dstep_ref, x_ref, dy_ref, w_ref, r_ref, prm_s, sel_s, step_s, decay_s, sig_s, within_s, wt_s, st_s, te_s, ew_s, tm_s, fm_s, l3_s, full_s,
    r_acc, c_acc, dl_acc, sk_acc, dxa, pr, pc, dri, dwi, xt_s,
    sd, got, back, cg, es, tb, tgot, cb, crow, py, pr_all, hy, hr,
    in_sem, out_sem, end_sem, s1, r1, s2, r2, s3, r3, s4, r4, py_s, py_r, pz_s, pz_r, hy_s, hy_r, hr_s, hr_r,
):
    c = lax.axis_index("seq")
    d = lax.axis_index("dp")
    loads = [
        pltpu.make_async_copy(a, b, in_sem.at[i])
        for i, (a, b) in enumerate(((x_hbm, x_ref), (dy_hbm, dy_ref), (w_hbm, w_ref), (r_hbm, r_ref)))
    ]
    for load in loads:
        load.start()

    y, row, rows = c % ROW, c // ROW, n // ROW
    gq = groups // ROW
    pq = gq * PAIRS
    po = pq // rows

    def in_row(t):
        return {"seq": row * ROW + t}

    def in_column(t):
        return {"seq": t * ROW + y}

    def in_cell(t):
        return {"seq": row * ROW + t // dps, "dp": t % dps}

    barrier = pltpu.get_barrier_semaphore()
    for i in range(1, rows):
        pl.semaphore_signal(barrier, inc=1, device_id=in_column((row + i) % rows), device_id_type=MESH)
    cell, at_cell = ROW * dps, y * dps + d
    for i in range(1, cell):
        pl.semaphore_signal(barrier, inc=1, device_id=in_cell((at_cell + i) % cell), device_id_type=MESH)
    for g in range(groups):
        one = spread(g, heads)
        sel_s[g, :heads] = one
        sel_s[g, heads:] = one
    for acc in (r_acc, c_acc, dl_acc, sk_acc):
        acc[...] = jnp.zeros_like(acc)
    pl.semaphore_wait(barrier, rows - 1 + cell - 1)

    lane = lax.broadcasted_iota(jnp.int32, (8, heads), 1)
    which = lax.broadcasted_iota(jnp.int32, (8, heads), 0)
    mine = jnp.zeros((8, heads), FL)
    owned = heads // n
    for i, ref in enumerate((bias_ref, dlog_ref, gain_ref)):
        for k in range(owned):
            mine = jnp.where((which == i) & (lane == c * owned + k), ref[k], mine)

    def total(value, buf, me, count, where, send, recv):
        buf[me] = value

        def copy(i, slot):
            return pltpu.make_async_remote_copy(
                src_ref=buf.at[slot], dst_ref=buf.at[slot], send_sem=send.at[i], recv_sem=recv.at[slot],
                device_id=where((me + i) % count), device_id_type=MESH,
            )

        for i in range(1, count):
            copy(i, me).start()
        for i in range(1, count):
            copy(i, (me + i) % count).wait_recv()
        out = jnp.sum(buf[...], axis=0)
        for i in range(1, count):
            copy(i, me).wait_send()
        return out

    mine = total(mine, py, y, ROW, in_row, py_s, py_r)
    prm_s[...] = total(mine, pr_all, row, rows, in_column, pz_s, pz_r)
    v, step, _, decay, within = rates(raw_ref[...], prm_s[...])
    within_s[...] = within
    step_s[...] = step
    last = within[BLOCK - 1 : BLOCK]
    te_s[...] = cat_hi_lo(jnp.exp(last - within) * step)
    l3_s[...] = last_terms(last)

    def rest():
        within, step = within_s[...], step_s[...]
        last, mid = within[BLOCK - 1 : BLOCK], within[HALF - 1 : HALF]
        wt_s[...] = within.T
        st_s[...] = step.T
        tm_s[...] = cat_hi_lo(jnp.exp(mid - within[:HALF]) * step[:HALF])
        fm_s[...] = cat_hi_lo(jnp.exp(within[HALF:] - mid))
        full_s[...] = cat_hi_lo(jnp.concatenate([jnp.exp(last), prm_s[2:3], jnp.zeros((6, heads), FL)], axis=0))

    for load in loads:
        load.wait()

    def span(half, k):
        return pl.ds(k * PAIRS * 128, PAIRS * 128 + (pq * DEC if half == 0 and k == gq - 1 else 0))

    def out(half, k, t, slot):
        at = span(half, k)
        return pltpu.make_async_remote_copy(
            src_ref=sd.at[half, t, at], dst_ref=got.at[half, slot, at],
            send_sem=s1.at[half, k, t], recv_sem=r1.at[half, k, slot], device_id=in_row(t), device_id_type=MESH,
        )

    def make(half, t, k):
        g = t * gq + k
        at = (half, t)
        src = (x_ref, te_s, w_ref) if half == 0 else (dy_ref, ew_s, r_ref)
        half_states(g, src[0], src[1][...], src[2], sel_s[g], sd.at[half, t, pl.ds(k * PAIRS * 128, PAIRS * 128)], (), xt_s if half == 0 else None)
        if half == 0:
            lx = dot(l3_s[...], sel_s[g, :heads]).astype(BF)
            for p in range(PAIRS):
                at = pq * 128 + (k * PAIRS + p) * DEC
                sd[0, t, at : at + DEC, :] = lx[:, p * 128 : p * 128 + 128]

    for half in range(2):
        if half == 1:
            ew_s[...] = cat_hi_lo(jnp.exp(within_s[...]))
            decay_s[...] = decay
            sig_s[...] = 1.0 / (1.0 + jnp.exp(-v))
        for k in range(gq):

            def send(i, _):
                t = (y + i) % ROW
                make(half, t, k)
                out(half, k, t, y).start()
                return 0

            lax.fori_loop(1, ROW, send, 0)
        for k in range(gq):
            make(half, y, k)
        got[half, y] = sd[half, y]

    def local(g, _):
        glanes = pl.ds(pl.multiple_of(g * NSTATE, NSTATE), NSTATE)
        sel2 = sel_s[g]
        dr_i, dw_i = intra(
            g, heads, x_ref, dy_ref, w_ref, r_ref, within_s[...], wt_s, st_s, tm_s[...], fm_s[...], dxa, pr, pc, sel2
        )
        lanes = pl.ds(pl.multiple_of(g * GW, GW), GW)
        dyf = dy_ref[:, lanes].astype(FL)
        dxa[:, lanes] += dot(full_s[...], sel2)[1:2] * dyf
        skips = jnp.sum(x_ref[:, lanes].astype(FL) * dyf, axis=0, keepdims=True)
        sk_acc[...] += gather_heads(jnp.broadcast_to(skips, (8, GW)), sel2[:heads])[0:1]
        dri[:, glanes] = dr_i
        dwi[:, glanes] = dw_i
        r_acc[...] += gather_heads(pr[...], sel2[:heads])
        c_acc[...] += gather_heads(pc[...], sel2[:heads])
        return 0

    rest()
    share = (groups * 5 // 8, groups * 6 // 8, groups * 7 // 8, groups)
    lax.fori_loop(0, share[0], local, 0)

    def arrived(half):
        for k in range(gq):
            for i in range(1, ROW):
                t = (y + i) % ROW
                out(half, k, t, t).wait_recv()

    def whole(p):
        return pl.ds(pl.multiple_of(p * 128, 128), 128)

    def up(half, src, t, slot):
        at = pl.ds(0, po * 128 + (po * DEC if half == 0 else 0))
        return pltpu.make_async_remote_copy(
            src_ref=src.at[half, t, at], dst_ref=tgot.at[half, slot, at],
            send_sem=s3.at[half, t], recv_sem=r3.at[half, slot], device_id=in_column(t), device_id_type=MESH,
        )

    def down(half, t, slot):
        return pltpu.make_async_remote_copy(
            src_ref=cb.at[half, t], dst_ref=crow.at[half, slot],
            send_sem=s4.at[half, t], recv_sem=r4.at[half, slot], device_id=in_column(t), device_id_type=MESH,
        )

    def ret(half, k, t, slot):
        at = pl.ds(pl.multiple_of(k * (PAIRS * 128), PAIRS * 128), PAIRS * 128)
        return pltpu.make_async_remote_copy(
            src_ref=back.at[half, t, at], dst_ref=cg.at[half, slot, at],
            send_sem=s2.at[half, k, t], recv_sem=r2.at[half, k, slot], device_id=in_row(t), device_id_type=MESH,
        )

    def blocks(half):
        return range(ROW) if half == 0 else range(ROW - 1, -1, -1)

    def log_decay(rows3):
        f = rows3.astype(FL)
        return f[0:1] + f[1:2] + f[2:3]

    def row_totals(half):
        arrived(half)

        def one(p, _):
            if half == 0:
                logs = jnp.zeros((1, 128), FL)
                for b in range(ROW):
                    log = log_decay(got[0, b, pl.ds(pl.multiple_of(pq * 128 + p * DEC, DEC), DEC), :])
                    es[b, p] = jnp.broadcast_to(jnp.exp(log), (8, 128))
                    logs += log
                h, m, l = three(logs)
                terms = jnp.concatenate([h, m, l, jnp.zeros((DEC - 3, 128), BF)], axis=0)
                tb[0, p // po, pl.ds(pl.multiple_of(po * 128 + (p % po) * DEC, DEC), DEC), :] = terms
            acc = jnp.zeros((128, 128), FL)
            for b in blocks(half):
                acc = acc * es[b, p, 0:1] + got[half, b, whole(p), :].astype(FL)
            tb[half, p // po, whole(p % po), :] = acc.astype(BF)
            return 0

        lax.fori_loop(0, pq, one, 0)
        for i in range(1, rows):
            up(half, tb, (row + i) % rows, row).start()
        tgot[half, row] = tb[half, row]

    def scan_rows(half):
        for i in range(1, rows):
            t = (row + i) % rows
            up(half, tb, t, t).wait_recv()
        for p in range(po):
            at = slice(p * 128, p * 128 + 128)

            def one(i, acc):
                t = i if half == 0 else rows - 1 - i
                cb[half, t, at, :] = acc.astype(BF)
                e = jnp.exp(log_decay(tgot[0, t, po * 128 + p * DEC : po * 128 + (p + 1) * DEC, :]))
                return acc * e + tgot[half, t, at, :].astype(FL)

            lax.fori_loop(0, rows, one, jnp.zeros((128, 128), FL))
        for i in range(1, rows):
            down(half, (row + i) % rows, row).start()
        crow[half, row] = cb[half, row]

    def scan_blocks(half):
        for i in range(1, rows):
            t = (row + i) % rows
            down(half, t, t).wait_recv()
        for k in range(gq):

            def one(i, _):
                p = k * PAIRS + i
                acc = crow[half, p // po, whole(p % po), :].astype(FL)
                for b in blocks(half):
                    back[half, b, whole(p), :] = acc.astype(BF)
                    acc = acc * es[b, p, 0:1] + got[half, b, whole(p), :].astype(FL)
                return 0

            lax.fori_loop(0, PAIRS, one, 0)
            if half == 0:
                for i in range(1, ROW):
                    ret(half, k, (y + i) % ROW, y).start()
            else:
                ret(half, k, (y + 2) % ROW, y).start()
        if half == 1:
            for k in range(gq):
                for i in (1, 3):
                    ret(half, k, (y + i) % ROW, y).start()
        cg[half, y] = back[half, y]

    row_totals(0)
    lax.fori_loop(share[0], share[1], local, 0)
    scan_rows(0)
    lax.fori_loop(share[1], share[2], local, 0)
    scan_blocks(0)
    row_totals(1)
    lax.fori_loop(share[2], share[3], local, 0)
    scan_rows(1)
    scan_blocks(1)

    def lane_cat(ref, half, t, k):
        return jnp.concatenate(
            [ref[half, t, pl.ds(pl.multiple_of((k * PAIRS + p) * 128, 128), 128), :] for p in range(PAIRS)], axis=1
        )

    def landed(half, k, t):
        @pl.when(t != y)
        def _():
            ret(half, k, t, t).wait_recv()

    def slices(g):
        return pl.ds(pl.multiple_of(g * GW, GW), GW), pl.ds(pl.multiple_of(g * NSTATE, NSTATE), NSTATE)

    def carried(j, _):
        k, t = j // ROW, (y + j) % ROW
        g = t * gq + k
        landed(0, k, t)
        lanes, glanes = slices(g)
        sel2 = sel_s[g]
        dyw = (dy_ref[:, lanes].astype(FL) * dot(ew_s[...], sel2)).astype(BF)
        car = lane_cat(cg, 0, t, k)
        r_acc[...] += gather_heads(dyw.astype(FL) * dot(r_ref[:, glanes], car), sel2[:heads])
        dr_ref[:, glanes] = (dri[:, glanes] + dot_nt(dyw, car)).astype(BF)
        return 0

    lax.fori_loop(0, groups, carried, 0)
    ends = [
        pltpu.make_async_copy(a, b, end_sem.at[i])
        for i, (a, b) in enumerate(((dr_ref, dr_hbm), (dw_ref, dw_hbm), (dstep_ref, ds_hbm)))
    ]
    ends[0].start()

    def returned(j, _):
        late = j // 4
        k = (1 - late) * (j % 2) + late * (j % 4 // 2)
        t = (y + (1 - late) * (j // 2 * 2) + late * (1 + j % 2 * 2)) % ROW
        g = t * gq + k
        landed(1, k, t)
        lanes, glanes = slices(g)
        sel2 = sel_s[g]
        sel = sel2[:heads]
        te = dot(te_s[...], sel2)
        xt = xt_s[:, lanes]
        ea = dot(full_s[...], sel2)[0:1]
        car, gst, own = lane_cat(cg, 0, t, k), lane_cat(cg, 1, t, k), lane_cat(sd, 0, t, k)
        zg = dot(w_ref[:, glanes], gst)
        c_acc[...] += gather_heads(xt.astype(FL) * zg, sel)
        ends = jnp.sum(gst.astype(FL) * (own.astype(FL) + ea * car.astype(FL)), axis=0, keepdims=True)
        dl_acc[...] += gather_heads(jnp.broadcast_to(ends, (8, GW)), sel)[0:1]
        dw_ref[:, glanes] = (dwi[:, glanes] + dot_nt(xt, gst)).astype(BF)
        xt_s[:, lanes] = (dxa[:, lanes] + te * zg).astype(BF)
        pltpu.make_async_copy(xt_s.at[:, lanes], dx_hbm.at[:, lanes], out_sem.at[g]).start()
        return 0

    lax.fori_loop(0, groups, returned, 0)
    ends[1].start()
    rate = -jnp.exp(prm_s[1:2])
    trow = lax.broadcasted_iota(jnp.int32, (BLOCK, heads), 0)
    dwithin = r_acc[...] - c_acc[...] + jnp.where(trow == BLOCK - 1, dl_acc[...], 0.0)
    dld = tri_sum(triangle(True), dwithin)
    draw = (c_acc[...] / step_s[...] + rate * dld) * sig_s[...]
    sums = jnp.concatenate(
        [
            jnp.sum(dld * decay_s[...], axis=0, keepdims=True),
            jnp.sum(draw, axis=0, keepdims=True),
            sk_acc[...],
            jnp.zeros((5, heads), FL),
        ],
        axis=0,
    )
    dstep_ref[...] = draw.astype(BF)
    ends[2].start()
    sums = total(sums, hy, at_cell, cell, in_cell, hy_s, hy_r)
    sums = total(sums, hr, row, rows, in_column, hr_s, hr_r) * factor
    hg_ref[...] = pltpu.roll(sums, lax.rem(heads - c * owned, heads), 1)
    for half in range(2):
        for i in range(1, ROW):
            for k in range(gq):
                out(half, k, (y + i) % ROW, y).wait_send()
                ret(half, k, (y + i) % ROW, y).wait_send()
        for i in range(1, rows):
            up(half, tb, (row + i) % rows, row).wait_send()
            down(half, (row + i) % rows, row).wait_send()

    def written(g, _):
        lanes = pl.ds(pl.multiple_of(g * GW, GW), GW)
        pltpu.make_async_copy(xt_s.at[:, lanes], dx_hbm.at[:, lanes], out_sem.at[g]).wait()
        return 0

    lax.fori_loop(0, groups, written, 0)
    for end in ends:
        end.wait()


def finish(
    owned, dx_in, dw_in, dr_in, ds_in, hg_in, dx_out, dw_out, dr_out, ds_out, hg_out, dx, dw, dr, ds, hg, own, sem
):
    step = BLOCK // PARTS
    parts = [pl.ds(i * step, step) for i in range(PARTS)]
    moves = [(hg_in, hg, hg_out)] + [(dx_in.at[p], dx.at[p], dx_out.at[p]) for p in parts]
    moves += [(dw_in, dw, dw_out), (dr_in, dr, dr_out), (ds_in, ds, ds_out)]
    loads = [pltpu.make_async_copy(a, b, sem.at[0, i]) for i, (a, b, _) in enumerate(moves)]
    stores = [
        pltpu.make_async_copy(own if i == 0 else b, c, sem.at[1, i]) for i, (_, b, c) in enumerate(moves)
    ]
    for load in loads:
        load.start()
    for i, (load, store) in enumerate(zip(loads, stores)):
        load.wait()
        if i == 0:
            own[...] = hg[:3, :owned]
        store.start()
    for store in stores:
        store.wait()


def body(head_inputs, write_proj, read_projection, step_raw, output_grad, decay_log, step_bias, skip_gain):
    n, dps = lax.axis_size("seq"), lax.axis_size("dp")
    x, w, r, raw, dy = head_inputs[0], write_proj[0], read_projection[0], step_raw[0], output_grad[0]
    heads = raw.shape[1]
    groups = heads // PER_GROUP
    owned = heads // n
    factor = 1.0 / math.sqrt(dps * n * BLOCK * HEADDIM)
    vm = pl.BlockSpec(memory_space=pltpu.VMEM)
    sm = pl.BlockSpec(memory_space=pltpu.SMEM)
    hbm = pl.BlockSpec(memory_space=pl.ANY)
    cat2 = pltpu.VMEM((BLOCK, 2 * heads), BF)
    cat1 = pltpu.VMEM((HALF, 2 * heads), BF)
    full = pltpu.VMEM((BLOCK, heads), FL)
    tr = pltpu.VMEM((heads, BLOCK), FL)
    row = pltpu.VMEM((1, heads), FL)
    wide = pltpu.VMEM((BLOCK, GW), FL)
    rows, gq = n // ROW, groups // ROW
    pq = gq * PAIRS
    po = pq // rows

    def small(count):
        return pltpu.VMEM((count, 8, heads), FL)

    sem = pltpu.SemaphoreType.DMA
    dx, dw, dr, dstep, hg = pl.pallas_call(
        functools.partial(kernel, heads, groups, n, dps, factor),
        out_shape=[
            jax.ShapeDtypeStruct(x.shape, BF),
            jax.ShapeDtypeStruct(w.shape, BF),
            jax.ShapeDtypeStruct(r.shape, BF),
            jax.ShapeDtypeStruct(raw.shape, BF),
            jax.ShapeDtypeStruct((8, heads), FL),
        ],
        in_specs=[hbm] * 4 + [vm] + [sm] * 3,
        out_specs=[hbm] * 4 + [vm],
        scratch_shapes=[
            pltpu.VMEM(w.shape, BF), pltpu.VMEM(r.shape, BF), pltpu.VMEM(raw.shape, BF),
            pltpu.VMEM(x.shape, BF), pltpu.VMEM(x.shape, BF), pltpu.VMEM(w.shape, BF), pltpu.VMEM(r.shape, BF),
            pltpu.VMEM((8, heads), FL), pltpu.VMEM((groups, 2 * heads, GW), BF), full, full, full,
            full, tr, tr, cat2, cat2, cat1, cat1,
            pltpu.VMEM((DEC, heads), BF), pltpu.VMEM((8, 2 * heads), BF),
            full, full, row, row,
            pltpu.VMEM(x.shape, FL), wide, wide, pltpu.VMEM(r.shape, FL), pltpu.VMEM(w.shape, FL), pltpu.VMEM(x.shape, BF),
            pltpu.VMEM((2, ROW, pq * 128 + pq * DEC, 128), BF), pltpu.VMEM((2, ROW, pq * 128 + pq * DEC, 128), BF),
            pltpu.VMEM((2, ROW, pq * 128, 128), BF), pltpu.VMEM((2, ROW, pq * 128, 128), BF),
            pltpu.VMEM((ROW, pq, 8, 128), FL),
            pltpu.VMEM((2, rows, po * (128 + DEC), 128), BF), pltpu.VMEM((2, rows, po * (128 + DEC), 128), BF),
            pltpu.VMEM((2, rows, po * 128, 128), BF), pltpu.VMEM((2, rows, po * 128, 128), BF),
            small(ROW), small(rows), small(ROW * dps), small(rows),
            sem((4,)), sem((groups,)), sem((3,)), sem((2, gq, ROW)), sem((2, gq, ROW)), sem((2, gq, ROW)), sem((2, gq, ROW)),
            sem((2, rows)), sem((2, rows)), sem((2, rows)), sem((2, rows)),
            sem((ROW,)), sem((ROW,)), sem((rows,)), sem((rows,)),
            sem((ROW * dps,)), sem((ROW * dps,)), sem((rows,)), sem((rows,)),
        ],
        compiler_params=pltpu.CompilerParams(
            collective_id=0, has_side_effects=True, vmem_limit_bytes=60 * 2**20
        ),
        name="mixer_backward",
    )(x, dy, w, r, raw, step_bias, decay_log, skip_gain)
    dx, dw, dr, dstep, hg = pl.pallas_call(
        functools.partial(finish, owned),
        out_shape=[jax.ShapeDtypeStruct(a.shape, BF) for a in (dx, dw, dr, dstep)]
        + [jax.ShapeDtypeStruct((3, owned), FL)],
        in_specs=[hbm] * 5,
        out_specs=[hbm] * 5,
        scratch_shapes=[pltpu.VMEM(a.shape, BF) for a in (dx, dw, dr, dstep)]
        + [pltpu.VMEM(hg.shape, FL), pltpu.VMEM((3, owned), FL), sem((2, 4 + PARTS))],
        name="results",
    )(dx, dw, dr, dstep, hg)
    return (dx[None], dw[None], dr[None], dstep[None], hg)


def solution(mesh):
    tok = P("dp", "seq", None)
    return jax.shard_map(
        body,
        mesh=mesh,
        in_specs=(tok, tok, tok, tok, tok, P("seq"), P("seq"), P("seq")),
        out_specs=(tok, tok, tok, tok, P(None, "seq")),
        check_vma=False,
    )
```
